32 devices in a mesh: row: 4 (over y, x), col: 4 (over z), lag: 2 (over core).
Axes of the slice: x: 2, y: 2, z: 4, core: 2. Of those that a mesh axis runs over, the one named last changes fastest.
Arguments:
- history: bfloat16 [8, 4, 128, 8192], P('lag', 'col', None, 'row'), may hold values from -6 to 6
- kernel_tiles: bfloat16 [4, 4, 8, 12, 256, 256], P('row', 'col', 'lag'), may hold values from -0.09375 to 0.09375
- tile_rows: int32 [4, 4, 8, 12], P('row', 'col', 'lag'), may hold values from 0 to 31
- tile_cols: int32 [4, 4, 8, 12], P('row', 'col', 'lag'), may hold values from 0 to 31
- tile_count: int32 [4, 4, 8], P('row', 'col', 'lag'), may hold values from 3 to 12, as said below
- base_stress: float32 [128, 32768], P(None, ('row', 'col', 'lag')), may hold values from -6 to 6
- prev_rate: float32 [128, 32768], P(None, ('row', 'col', 'lag')), may hold values from -6 to 6
- direct_effect: float32 [128, 32768], P(None, ('row', 'col', 'lag')), may hold values from 0.5 to 2
- state_var: float32 [128, 32768], P(None, ('row', 'col', 'lag')), may hold values from -2 to 2
Outputs:
- stress_change: float32 [128, 32768], P(None, ('row', 'col', 'lag'))
- new_rate: float32 [128, 32768], P(None, ('row', 'col', 'lag'))
The draws below stay inside these ranges and needn't reach their ends.
Inputs may be any that keep to these rules, and one draw needn't show every extreme that they name: `tile_count`: every draw has some device and lag with all 12 slots live.
All inputs are finite; a program needn't handle non-finite values.
Results may differ from the reference program's by a relative error of at most 0.0003.
Values may be sent and summed in bfloat16 or wider, within the bound.
No kernel may reach another device: no remote copies, remote signals or barrier semaphores. Data moves between devices by JAX's collectives and lax.ppermute only.
A program may use at most 64 MiB of HBM per device.

```python
import math
import jax
import jax.numpy as jnp
from jax import lax

TILE = 256
REC_DEV = 8192
SIMS = 128
LAGS = 8
NT = 12
NEWTON = 4
ELEMS = 32768
SRC_DEV = 8192
RB = 32
CB = 32
N_ROW = 4
N_COL = 4


def draw_tile_count(key, part):
    first_key, second_key = jax.random.split(jax.random.fold_in(key, 17))
    counts = jax.random.randint(first_key, (N_ROW * N_COL * LAGS,), max(1, NT // 4), NT + 1)
    chosen = jax.random.randint(second_key, (), 0, N_ROW * N_COL * LAGS)
    counts = jnp.where(jnp.arange(N_ROW * N_COL * LAGS) == chosen, NT, counts)
    return counts.reshape(N_ROW, N_COL, LAGS).astype(jnp.int32)


def touch_ends(entries, key, least, largest):
    spot = [jax.random.randint(jax.random.fold_in(key, axis), (), 0, length) for axis, length in enumerate(entries.shape)]
    widest = entries.shape.index(max(entries.shape))
    beside = spot[:widest] + [(spot[widest] + 1) % entries.shape[widest]] + spot[widest + 1:]
    return entries.at[tuple(spot)].set(least).at[tuple(beside)].set(largest)


def block_scale(stream_key, extent, pieces, smallest, largest):
    def one(axis_at, blocks):
        heights = jax.random.uniform(jax.random.fold_in(jax.random.fold_in(stream_key, 6), axis_at), (blocks,), jnp.float32, smallest / len(pieces), largest / len(pieces))
        return jnp.repeat(jnp.exp(heights), extent[axis_at] // blocks).reshape((-1,) + (1,) * (len(extent) - axis_at - 1))

    level = one(*pieces[0])
    for cut in pieces[1:]:
        level = level * one(*cut)
    return level


def bell_draw(own_key, shape, deviation, most, shards=(), held_as=jnp.bfloat16):
    entries = jax.random.normal(own_key, shape, jnp.float32) * deviation
    if len(shards) > 0:
        entries = block_scale(own_key, shape, shards, -0.22, 0.18) * entries
    return jnp.clip(entries, min=-most, max=most).astype(held_as)


def setup_inputs(seed: int = 0) -> dict:
    key_list = jax.random.split(jax.random.key(seed), 10)
    history = bell_draw(key_list[0], (LAGS, N_COL, SIMS, SRC_DEV), 1.0, 6.0, ((0, 2), (1, 4), (3, 4)))
    kernel_tiles = bell_draw(key_list[1], (N_ROW, N_COL, LAGS, NT, TILE, TILE), (TILE * LAGS * N_COL // 2) ** -0.5, 0.09375, ((0, 4), (1, 4), (2, 2)))
    tile_rows = touch_ends(jax.random.randint(key_list[2], (N_ROW, N_COL, LAGS, NT), 0, RB), jax.random.fold_in(key_list[2], 1), 0, RB - 1).astype(jnp.int32)
    tile_cols = touch_ends(jax.random.randint(key_list[3], (N_ROW, N_COL, LAGS, NT), 0, CB), jax.random.fold_in(key_list[3], 1), 0, CB - 1).astype(jnp.int32)
    tile_count = draw_tile_count(jax.random.fold_in(key_list[9], 71), 0)
    base_stress = bell_draw(key_list[5], (SIMS, ELEMS), 1.0, 6.0, ((1, 32),), jnp.float32)
    prev_rate = bell_draw(key_list[6], (SIMS, ELEMS), 1.0, 6.0, ((1, 32),), jnp.float32)
    direct_effect = jnp.clip(jnp.exp(math.log(2.0) - 1.3862944 * jax.random.uniform(key_list[7], (SIMS, ELEMS), jnp.float32) ** block_scale(key_list[7], (SIMS, ELEMS), ((1, 32),), -0.2, 0.2)), 0.5, 2.0)
    state_var = jnp.clip(jax.random.uniform(key_list[8], (SIMS, ELEMS), jnp.float32, -2.0, 2.0) * block_scale(key_list[8], (SIMS, ELEMS), ((1, 32),), -0.4, 0.0), -2.0, 2.0)
    return dict(history=history, kernel_tiles=kernel_tiles, tile_rows=tile_rows, tile_cols=tile_cols, tile_count=tile_count, base_stress=base_stress, prev_rate=prev_rate, direct_effect=direct_effect, state_var=state_var)


def inverse_sinh(value):
    magnitude = jnp.abs(value)
    return jnp.sign(value) * jnp.log(magnitude + jnp.sqrt(1.0 + magnitude * magnitude))

def reference(history, kernel_tiles, tile_rows, tile_cols, tile_count, base_stress, prev_rate, direct_effect, state_var):
    col_blocks = SRC_DEV // TILE
    row_blocks = REC_DEV // TILE

    def one_row(row_index):

        def one_col(running, col_index):
            blocks = history[:, col_index].astype(jnp.float32).reshape(LAGS, SIMS, col_blocks, TILE)
            choose = jax.nn.one_hot(tile_cols[row_index, col_index], col_blocks, dtype=jnp.float32)
            picked = jnp.einsum('lkb,lsbj->lksj', choose, blocks, precision=lax.Precision.HIGHEST)
            weights = kernel_tiles[row_index, col_index].astype(jnp.float32)
            contrib = jnp.einsum('lksj,lkij->lksi', picked, weights, precision=lax.Precision.HIGHEST)
            alive_mask = (jnp.arange(NT)[None, :] < tile_count[row_index, col_index][:, None]).astype(jnp.float32)
            placing = jax.nn.one_hot(tile_rows[row_index, col_index], row_blocks, dtype=jnp.float32) * alive_mask[:, :, None]
            added = jnp.einsum('lkb,lksi->sbi', placing, contrib, precision=lax.Precision.HIGHEST)
            return (running + added.reshape(SIMS, REC_DEV), None)
        summed, unused = lax.scan(one_col, jnp.zeros((SIMS, REC_DEV), jnp.float32), jnp.arange(N_COL))
        return summed
    blocks_all = lax.map(one_row, jnp.arange(N_ROW))
    stress_change = jnp.transpose(blocks_all, (1, 0, 2)).reshape(SIMS, N_ROW * REC_DEV)
    driving = base_stress + stress_change
    factor = jnp.exp(state_var) / 2.0
    velocity = prev_rate
    for step in range(NEWTON):
        scaled = velocity * factor
        misfit = direct_effect * inverse_sinh(scaled) + 0.5 * velocity - driving
        slope = direct_effect * factor / jnp.sqrt(1.0 + scaled * scaled) + 0.5
        velocity = velocity - misfit / slope
    return (stress_change, velocity)
```

```python
import functools

import jax
import jax.numpy as jnp
from jax import lax
from jax.experimental import pallas as pl
from jax.experimental.pallas import tpu as pltpu
from jax.sharding import PartitionSpec as P

NEWTON = 4
CAP = 16
PAD = 16
VMEM_LIMIT = 48 * 1024 * 1024
ANY = pl.BlockSpec(memory_space=pl.ANY)
SMEM = pl.BlockSpec(memory_space=pltpu.SMEM)


def inverse_sinh(value):
    magnitude = jnp.abs(value)
    length = jnp.log(magnitude + jnp.sqrt(1.0 + magnitude * magnitude))
    return jnp.where(value < 0.0, -length, length)


def friction(stress, base, velocity, direct, state):
    driving = base + stress
    factor = jnp.exp(state) / 2.0
    gain = direct * factor
    for step in range(NEWTON):
        scaled = velocity * factor
        misfit = direct * inverse_sinh(scaled) + 0.5 * velocity - driving
        slope = gain / jnp.sqrt(1.0 + scaled * scaled) + 0.5
        velocity = velocity - misfit / slope
    return velocity


def partners(size, step):
    return [(index, index ^ step) for index in range(size)]


def pack_kernel(cap, row_ref, *refs):
    peers = (len(refs) - 2) // 2
    needs, history, packed, sems = refs[:peers], refs[peers], refs[peers + 1 : -1], refs[-1]
    lags, _, sims, width = history.shape
    side = packed[0].shape[2]
    local_blocks = width // side
    total = needs[0].shape[0] // lags
    first = row_ref[0] * local_blocks
    counts = []
    for peer in range(peers):

        def visit(step, position, peer=peer):
            lag = step // local_blocks
            block = step % local_blocks
            wanted = jnp.logical_and(
                needs[peer][lag * total + first + block] > 0, position < cap
            )

            @pl.when(wanted)
            def _():
                pltpu.make_async_copy(
                    history.at[lag, 0, :, pl.ds(pl.multiple_of(block * side, side), side)],
                    packed[peer].at[position],
                    sems.at[peer, position],
                ).start()

            return position + wanted.astype(jnp.int32)

        counts.append(lax.fori_loop(0, lags * local_blocks, visit, jnp.int32(0)))
    for peer in range(peers):

        def settle(position, carry, peer=peer):
            pltpu.make_async_copy(
                history.at[0, 0, :, pl.ds(0, side)], packed[peer].at[position], sems.at[peer, position]
            ).wait()
            return carry

        lax.fori_loop(0, counts[peer], settle, 0)


def pack(row, needs, history, side, cap):
    sims = history.shape[2]
    return pl.pallas_call(
        functools.partial(pack_kernel, cap),
        out_shape=[jax.ShapeDtypeStruct((cap, sims, side), history.dtype)] * len(needs),
        in_specs=[SMEM] * (1 + len(needs)) + [ANY],
        out_specs=[ANY] * len(needs),
        scratch_shapes=[pltpu.SemaphoreType.DMA((len(needs), cap))],
        compiler_params=pltpu.CompilerParams(vmem_limit_bytes=VMEM_LIMIT),
        name="pack_history",
    )(row, *needs, history)


def tiles_kernel(cap, where_ref, cols, rows, counts, places, *refs):
    kept, given, blocks, weights, sums, block_sems, weight_sems, out_sems = refs[-8:]
    tiles, history, received = refs[0], refs[1], refs[2:-8]
    _, _, lags, slots, side, _ = tiles.shape
    local_blocks = history.shape[3] // side
    total = places.shape[0] // lags
    _, col_size, per_owner, sims, _ = sums.shape
    row, core = where_ref[0], where_ref[1]

    def copies(lag, slot):
        index = lag * slots + slot
        col = cols[index]
        relative = lax.bitwise_xor(col // local_blocks, row)
        place = jnp.minimum(places[lag * total + col], cap - 1)
        local = pl.multiple_of((col % local_blocks) * side, side)
        return index, relative, place, local

    for lag in range(lags):

        def begin(slot, carry, lag=lag):
            index, relative, place, local = copies(lag, slot)
            pltpu.make_async_copy(
                tiles.at[0, 0, lag, slot], weights.at[index], weight_sems.at[index]
            ).start()

            @pl.when(relative == 0)
            def _():
                pltpu.make_async_copy(
                    history.at[lag, 0, :, pl.ds(local, side)], blocks.at[index], block_sems.at[index]
                ).start()

            for peer in range(len(received)):

                @pl.when(relative == peer + 1)
                def _(peer=peer):
                    pltpu.make_async_copy(
                        received[peer].at[place], blocks.at[index], block_sems.at[index]
                    ).start()

            return carry

        lax.fori_loop(0, counts[lag], begin, 0)
    sums[...] = jnp.zeros_like(sums)
    for lag in range(lags):

        def multiply(slot, carry, lag=lag):
            index = lag * slots + slot
            pltpu.make_async_copy(
                tiles.at[0, 0, lag, slot], weights.at[index], weight_sems.at[index]
            ).wait()
            pltpu.make_async_copy(
                history.at[lag, 0, :, pl.ds(0, side)], blocks.at[index], block_sems.at[index]
            ).wait()
            owner = rows[index] // per_owner
            other = lax.bitwise_xor(owner % 2, core)
            spot = (other, owner // 2, rows[index] % per_owner)
            sums[spot] += lax.dot_general(
                blocks[index],
                weights[index],
                (((1,), (1,)), ((), ())),
                preferred_element_type=jnp.float32,
            )
            return carry

        lax.fori_loop(0, counts[lag], multiply, 0)
    to_give = pltpu.make_async_copy(sums.at[1], given, out_sems.at[0])
    to_keep = pltpu.make_async_copy(sums.at[0], kept, out_sems.at[1])
    to_give.start()
    to_keep.start()
    to_give.wait()
    to_keep.wait()


def multiply_tiles(where, cols, rows, counts, places, tiles, history, received, col_size, per_owner, cap):
    _, _, lags, slots, side, _ = tiles.shape
    sims = history.shape[2]
    half = jax.ShapeDtypeStruct((col_size, per_owner, sims, side), jnp.float32)
    count = lags * slots
    return pl.pallas_call(
        functools.partial(tiles_kernel, cap),
        out_shape=[half, half],
        in_specs=[SMEM] * 5 + [ANY] * (2 + len(received)),
        out_specs=[ANY, ANY],
        scratch_shapes=[
            pltpu.VMEM((count, sims, side), history.dtype),
            pltpu.VMEM((count, side, side), tiles.dtype),
            pltpu.VMEM((2,) + half.shape, jnp.float32),
            pltpu.SemaphoreType.DMA((count,)),
            pltpu.SemaphoreType.DMA((count,)),
            pltpu.SemaphoreType.DMA((2,)),
        ],
        compiler_params=pltpu.CompilerParams(vmem_limit_bytes=VMEM_LIMIT),
        name="multiply_tiles",
    )(where, cols, rows, counts, places, tiles, history, *received)


def code_kernel(col_ref, kept, got, *refs):
    left, right, staged, total, in_sems, out_sems, own_sem = refs[-7:]
    own, coded = refs[0], refs[1:-7]
    col_size, per_owner, sims, side = kept.shape
    col = col_ref[0]
    reads = []
    for step in list(range(1, col_size)) + [0]:
        chunk = lax.bitwise_xor(col, step)
        pair = (
            pltpu.make_async_copy(kept.at[chunk], left.at[step], in_sems.at[0, step]),
            pltpu.make_async_copy(got.at[chunk], right.at[step], in_sems.at[1, step]),
        )
        for copy in pair:
            copy.start()
        reads.append((step, pair))
    writes = []
    for step, pair in reads:
        for copy in pair:
            copy.wait()
        if step == 0:
            total[...] = left[0] + right[0]
            writes.append(pltpu.make_async_copy(total, own, own_sem))
        else:
            slot = step - 1
            exponents = []
            for block in range(per_owner):
                value = left[step, block] + right[step, block]
                largest = jnp.maximum(jnp.max(jnp.abs(value), axis=0, keepdims=True), 1e-30)
                exponent = jnp.ceil(jnp.log2(largest))
                grid = jnp.clip(jnp.round(value * jnp.exp2(15.0 - exponent)), -32767.0, 32767.0)
                staged[slot, pl.ds(block * sims, sims), :] = grid.astype(jnp.int32).astype(jnp.int16)
                exponents.append(exponent)
            if per_owner < PAD:
                exponents.append(jnp.zeros((PAD - per_owner, side), jnp.float32))
            rows = jnp.concatenate(exponents, axis=0)
            staged[slot, pl.ds(per_owner * sims, PAD), :] = rows.astype(jnp.int32).astype(jnp.int16)
            writes.append(pltpu.make_async_copy(staged.at[slot], coded[slot], out_sems.at[slot]))
        writes[-1].start()
    for copy in writes:
        copy.wait()


def code(col, kept, got):
    col_size, per_owner, sims, side = kept.shape
    rows = per_owner * sims + PAD
    chunk = jax.ShapeDtypeStruct((rows, side), jnp.int16)
    return pl.pallas_call(
        code_kernel,
        out_shape=[jax.ShapeDtypeStruct(kept.shape[1:], jnp.float32)] + [chunk] * (col_size - 1),
        in_specs=[SMEM, ANY, ANY],
        out_specs=[ANY] * col_size,
        scratch_shapes=[
            pltpu.VMEM(kept.shape, jnp.float32),
            pltpu.VMEM(kept.shape, jnp.float32),
            pltpu.VMEM((col_size - 1, rows, side), jnp.int16),
            pltpu.VMEM(kept.shape[1:], jnp.float32),
            pltpu.SemaphoreType.DMA((2, col_size)),
            pltpu.SemaphoreType.DMA((col_size - 1,)),
            pltpu.SemaphoreType.DMA,
        ],
        compiler_params=pltpu.CompilerParams(vmem_limit_bytes=VMEM_LIMIT),
        name="add_and_code",
    )(col, kept, got)


def solve_kernel(per_owner, *refs):
    base, rate, direct, state, own = refs[:5]
    stress_out, rate_out = refs[-2:]
    codes = refs[5:-2]
    block = pl.program_id(0)
    stress = own[0]
    for index in range(len(codes) // 2):
        values, exponents = codes[2 * index], codes[2 * index + 1]
        powers = exponents[...].astype(jnp.int32).astype(jnp.float32)
        chosen = lax.broadcasted_iota(jnp.int32, powers.shape, 0) == block
        power = jnp.sum(jnp.where(chosen, powers, 0.0), axis=0, keepdims=True)
        stress = stress + values[...].astype(jnp.int32).astype(jnp.float32) * jnp.exp2(power - 15.0)
    stress_out[...] = stress
    rate_out[...] = friction(stress, base[...], rate[...], direct[...], state[...])


def solve(base, rate, direct, state, own, coded):
    per_owner, sims, side = own.shape
    wide = pl.BlockSpec((sims, side), lambda block: (0, block))
    specs = [wide] * 4 + [pl.BlockSpec((1, sims, side), lambda block: (block, 0, 0))]
    operands = [base, rate, direct, state, own]
    behind = per_owner * sims // PAD
    for chunk in coded:
        specs += [
            pl.BlockSpec((sims, side), lambda block: (block, 0)),
            pl.BlockSpec((PAD, side), lambda block: (behind, 0)),
        ]
        operands += [chunk, chunk]
    return pl.pallas_call(
        functools.partial(solve_kernel, per_owner),
        grid=(per_owner,),
        out_shape=[jax.ShapeDtypeStruct(base.shape, jnp.float32)] * 2,
        in_specs=specs,
        out_specs=[wide, wide],
        compiler_params=pltpu.CompilerParams(vmem_limit_bytes=VMEM_LIMIT),
        name="friction_solve",
    )(*operands)


def general(history, kernel_tiles, tile_rows, tile_cols, tile_count, base_stress, prev_rate, direct_effect, state_var):
    gathered = lax.all_gather(history, "row", axis=3, tiled=True)
    lag_local = gathered.shape[0]
    sims_count = gathered.shape[2]
    tile_side = kernel_tiles.shape[4]
    slots = kernel_tiles.shape[3]
    col_blocks = gathered.shape[3] // tile_side
    blocks = gathered.reshape(lag_local, sims_count, col_blocks, tile_side)
    choose = jax.nn.one_hot(tile_cols[0, 0], col_blocks, dtype=jnp.bfloat16)
    picked = jnp.einsum(
        "lkb,lsbj->lksj", choose, blocks, preferred_element_type=jnp.float32
    ).astype(jnp.bfloat16)
    contrib = jnp.einsum(
        "lksj,lkij->slki", picked, kernel_tiles[0, 0], preferred_element_type=jnp.float32
    )
    owned = base_stress.shape[1]
    rec_local = owned * lax.axis_size(("col", "lag"))
    row_blocks = rec_local // tile_side
    alive_mask = (jnp.arange(slots)[None, :] < tile_count[0, 0][:, None]).astype(jnp.float32)
    masked = (contrib * alive_mask[None, :, :, None]).reshape(
        sims_count, lag_local * slots, tile_side
    )
    targets = tile_rows[0, 0].reshape(lag_local * slots)
    placed = (
        jnp.zeros((sims_count, row_blocks, tile_side), jnp.float32).at[:, targets, :].add(masked)
    )
    summed = lax.psum(placed.reshape(sims_count, rec_local), ("col", "lag"))
    offset = lax.axis_index(("col", "lag")) * owned
    stress = lax.dynamic_slice_in_dim(summed, offset, owned, 1)
    return stress, friction(stress, base_stress, prev_rate, direct_effect, state_var)


def local(history, kernel_tiles, tile_rows, tile_cols, tile_count, base_stress, prev_rate, direct_effect, state_var):
    _, _, lags, slots, side, _ = kernel_tiles.shape
    row_size, col_size, core_size = (lax.axis_size(axis) for axis in ("row", "col", "lag"))
    row, col, core = (lax.axis_index(axis).astype(jnp.int32) for axis in ("row", "col", "lag"))
    local_blocks = history.shape[3] // side
    total = row_size * local_blocks
    per_owner = base_stress.shape[1] // side
    cap = min(CAP, lags * local_blocks)

    live = jnp.arange(slots)[None, :] < tile_count[0, 0][:, None]
    hits = (tile_cols[0, 0][:, :, None] == jnp.arange(total)[None, None, :]) & live[:, :, None]
    need = jnp.any(hits, axis=1).astype(jnp.int32)
    request = need.reshape(lags * total)
    requests = [lax.ppermute(request, "row", partners(row_size, step)) for step in range(1, row_size)]
    packed = pack(row[None], requests, history, side, cap)
    received = [
        lax.ppermute(packed[step - 1], "row", partners(row_size, step)) for step in range(1, row_size)
    ]

    by_owner = need.reshape(lags, row_size, local_blocks).transpose(1, 0, 2).reshape(row_size, -1)
    before = jnp.arange(lags * local_blocks)
    places = jnp.sum(
        jnp.where(before[None, None, :] < before[None, :, None], by_owner[:, None, :], 0), axis=2
    )
    places = places.reshape(row_size, lags, local_blocks).transpose(1, 0, 2).reshape(lags * total)
    elsewhere = jnp.arange(row_size) != row
    over = jnp.any((jnp.sum(by_owner, axis=1) > cap) & elsewhere)
    overflow = lax.pmax(over.astype(jnp.float32), ("row", "col", "lag"))

    kept, given = multiply_tiles(
        jnp.stack([row, core]),
        tile_cols.reshape(-1),
        tile_rows.reshape(-1),
        tile_count.reshape(-1),
        places,
        kernel_tiles,
        history,
        received,
        col_size,
        per_owner,
        cap,
    )
    got = lax.ppermute(given, "lag", partners(core_size, 1))
    own, *coded = code(col[None], kept, got)
    arrived = [
        lax.ppermute(coded[step - 1], "col", partners(col_size, step)) for step in range(1, col_size)
    ]
    stress, rate = solve(base_stress, prev_rate, direct_effect, state_var, own, arrived)
    return lax.cond(
        overflow > 0.0,
        lambda: general(
            history, kernel_tiles, tile_rows, tile_cols, tile_count, base_stress, prev_rate, direct_effect, state_var
        ),
        lambda: (stress, rate),
    )


def solution(mesh):
    return jax.shard_map(
        local,
        mesh=mesh,
        in_specs=(
            P("lag", "col", None, "row"),
            P("row", "col", "lag", None, None, None),
            P("row", "col", "lag", None),
            P("row", "col", "lag", None),
            P("row", "col", "lag"),
            P(None, ("row", "col", "lag")),
            P(None, ("row", "col", "lag")),
            P(None, ("row", "col", "lag")),
            P(None, ("row", "col", "lag")),
        ),
        out_specs=(P(None, ("row", "col", "lag")), P(None, ("row", "col", "lag"))),
        check_vma=False,
    )
```

```python
import functools
import math

import jax
import jax.numpy as jnp
from jax import lax
from jax.experimental import pallas as pl
from jax.experimental.pallas import tpu as pltpu
from jax.sharding import PartitionSpec as P

NEWTON = 4
CAP = 16
FIRST = 4
PAD = 16
LANES = 128
GROUP = 4
ANY = pl.BlockSpec(memory_space=pl.ANY)
SMEM = pl.BlockSpec(memory_space=pltpu.SMEM)
VMEM = pl.BlockSpec(memory_space=pltpu.VMEM)


def params(*shapes):
    held = sum(math.prod(s.shape) * jnp.dtype(s.dtype).itemsize for s in shapes)
    return pltpu.CompilerParams(vmem_limit_bytes=held + 8 * 1024 * 1024)


def partners(size, step):
    return [(index, index ^ step) for index in range(size)]


def inverse_sinh(value, root):
    length = jnp.log(jnp.abs(value) + root)
    return jnp.where(value < 0.0, -length, length)


def friction(stress, base, velocity, direct, state):
    driving = base + stress
    factor = jnp.exp(state) / 2.0
    gain = direct * factor
    for step in range(NEWTON):
        scaled = velocity * factor
        root = jnp.sqrt(1.0 + scaled * scaled)
        misfit = direct * inverse_sinh(scaled, root) + 0.5 * velocity - driving
        velocity = velocity - misfit / (gain / root + 0.5)
    return velocity


def request_kernel(cols, counts, need):
    lags, total = need.shape
    slots = cols.shape[3]
    names = lax.broadcasted_iota(jnp.int32, (1, total), 1)
    for lag in range(lags):
        marks = jnp.zeros((1, total), jnp.int32)
        for slot in range(slots):
            marks = jnp.where(
                (names == cols[0, 0, lag, slot]) & (slot < counts[0, 0, lag]), 1, marks
            )
        need[lag : lag + 1, :] = marks


def make_request(cols, counts, total):
    return pl.pallas_call(
        request_kernel,
        out_shape=jax.ShapeDtypeStruct((cols.shape[2], total), jnp.int32),
        in_specs=[SMEM, SMEM],
        out_specs=VMEM,
        name="mark_blocks",
    )(cols, counts)


def load_kernel(history, held, sem):
    copy = pltpu.make_async_copy(history, held, sem)
    copy.start()
    copy.wait()


def load(history):
    return pl.pallas_call(
        load_kernel,
        out_shape=history,
        in_specs=[ANY],
        out_specs=VMEM,
        scratch_shapes=[pltpu.SemaphoreType.DMA],
        compiler_params=params(history),
        name="load_history",
    )(history)


def pack_kernel(cap, pieces, side, where, *refs):
    peers = (len(refs) - 1) // (len(pieces) + 1)
    needs, history, packed = refs[:peers], refs[peers], refs[peers + 1 :]
    lags, sims, width = history.shape
    local_blocks = width // side
    first = where[0] * local_blocks
    for peer in range(peers):
        position = jnp.int32(0)
        for lag in range(lags):
            for block in range(local_blocks):
                wanted = needs[peer][lag, first + block]

                @pl.when((wanted > 0) & (position < cap))
                def _(peer=peer, lag=lag, block=block, position=position):
                    for piece, (begin, part) in enumerate(pieces):
                        packed[piece * peers + peer][position] = history[
                            lag, begin : begin + part, block * side : (block + 1) * side
                        ]

                position = position + wanted


def pack(where, needs, history, side, cap, pieces):
    outs = []
    for _, part in pieces:
        outs += [jax.ShapeDtypeStruct((cap, part, side), history.dtype)] * len(needs)
    return pl.pallas_call(
        functools.partial(pack_kernel, cap, pieces, side),
        out_shape=outs,
        in_specs=[SMEM] * (1 + len(needs)) + [VMEM],
        out_specs=[VMEM] * len(outs),
        compiler_params=params(history, *outs),
        name="pack_history",
    )(where, *needs, history)


def plan_kernel(cap, col_size, per_owner, where, cols, rows, counts, *refs):
    needs, tiles, (table, size, over, held, places, sem) = refs[:-7], refs[-7], refs[-6:]
    lags, total = needs[0].shape
    row, core = where[0], where[2]
    members = len(needs)
    started = jnp.int32(0)
    for lag in range(lags):

        def begin(slot, started, lag=lag):
            pltpu.make_async_copy(tiles.at[lag, slot], held.at[started], sem.at[started]).start()
            return started + 1

        started = lax.fori_loop(0, counts[0, 0, lag], begin, started)
    local_blocks = total // members
    for owner in range(members):
        position = jnp.int32(0)
        for lag in range(lags):
            for block in range(owner * local_blocks, (owner + 1) * local_blocks):
                places[lag, block] = position
                position = position + needs[0][lag, block]
    above = jnp.int32(0)
    for member in range(members):
        for owner in range(members):

            def count(block, wanted, member=member, owner=owner):
                for lag in range(lags):
                    wanted = wanted + needs[member][lag, owner * local_blocks + block]
                return wanted

            wanted = lax.fori_loop(0, local_blocks, count, jnp.int32(0))
            foreign = lax.bitwise_xor(row, member) != owner
            above = jnp.where(foreign & (wanted > cap), 1, above)
    over[0] = above
    filled = jnp.int32(0)
    for lag in range(lags):

        def note(slot, filled, lag=lag):
            col = cols[0, 0, lag, slot]
            target = rows[0, 0, lag, slot]
            owner = target // per_owner
            half = lax.bitwise_xor(owner % 2, core) * col_size + owner // 2
            table[0, filled] = lag
            table[1, filled] = lax.bitwise_xor(col // local_blocks, row)
            table[2, filled] = col % local_blocks
            table[3, filled] = jnp.minimum(places[lag, col], cap - 1)
            table[4, filled] = half * per_owner + target % per_owner
            return filled + 1

        filled = lax.fori_loop(0, counts[0, 0, lag], note, filled)
    size[0] = filled

    def settle(index, carry):
        pltpu.make_async_copy(tiles.at[0, 0], held.at[index], sem.at[index]).wait()
        return carry

    lax.fori_loop(0, filled, settle, 0)


def make_plan(where, cols, rows, counts, needs, tiles, cap, col_size, per_owner):
    lags, total = needs[0].shape
    count = lags * cols.shape[3]
    held = jax.ShapeDtypeStruct((count,) + tiles.shape[2:], tiles.dtype)
    return pl.pallas_call(
        functools.partial(plan_kernel, cap, col_size, per_owner),
        out_shape=[
            jax.ShapeDtypeStruct((5, count), jnp.int32),
            jax.ShapeDtypeStruct((1,), jnp.int32),
            jax.ShapeDtypeStruct((1,), jnp.int32),
            held,
        ],
        in_specs=[SMEM] * (4 + len(needs)) + [ANY],
        out_specs=[SMEM] * 3 + [VMEM],
        scratch_shapes=[pltpu.SMEM((lags, total), jnp.int32), pltpu.SemaphoreType.DMA((count,))],
        compiler_params=params(held),
        name="plan_tiles",
    )(where, cols, rows, counts, *needs, tiles)


def tiles_kernel(first, whole, extra, over, table, size, tiles, history, *refs):
    received, (kept, given, blocks, sums) = refs[: len(refs) - 4 - extra], refs[-4:]
    side = tiles.shape[2]
    halves, part, _ = sums.shape
    live = size[0]
    sums[...] = jnp.zeros_like(sums)

    def fetch(index, carry):
        lag, relative = table[0, index], table[1, index]
        lanes = pl.ds(pl.multiple_of(table[2, index] * side, side), side)

        @pl.when(relative == 0)
        def _():
            blocks[index] = history[lag, pl.ds(first, part), lanes]

        for peer in range(len(received)):

            @pl.when(relative == peer + 1)
            def _(peer=peer):
                if whole:
                    blocks[index] = received[peer][lag, pl.ds(first, part), lanes]
                else:
                    blocks[index] = received[peer][table[3, index]]

        return carry

    lax.fori_loop(0, live, fetch, 0)

    def multiply(group, carry):
        products = []
        for offset in range(GROUP):
            index = jnp.minimum(group * GROUP + offset, live - 1)
            products.append(
                lax.dot_general(
                    blocks[index], tiles[index], (((1,), (1,)), ((), ())), preferred_element_type=jnp.float32
                )
            )
        for offset, product in enumerate(products):
            index = group * GROUP + offset
            spot = table[4, jnp.minimum(index, live - 1)]
            sums[spot] += product if offset == 0 else jnp.where(index < live, product, 0.0)
        return carry

    lax.fori_loop(0, (live + GROUP - 1) // GROUP, multiply, 0)
    kept[...] = sums[: halves // 2]
    given[: halves // 2] = sums[halves // 2 :]
    given[halves // 2] = jnp.full((part, side), 1.0, jnp.float32) * over[0].astype(jnp.float32)


def multiply_tiles(first, part, whole, over, table, size, tiles, history, received, chunks, after):
    side = tiles.shape[2]
    half = jax.ShapeDtypeStruct((chunks, part, side), jnp.float32)
    more = jax.ShapeDtypeStruct((chunks + 1, part, side), jnp.float32)
    blocks = pltpu.VMEM((table.shape[1], part, side), history.dtype)
    sums = pltpu.VMEM((2 * chunks, part, side), jnp.float32)
    return pl.pallas_call(
        functools.partial(tiles_kernel, first, whole, len(after)),
        out_shape=[half, more],
        in_specs=[SMEM] * 3 + [VMEM] * (2 + len(received)) + [ANY] * len(after),
        out_specs=[VMEM, VMEM],
        scratch_shapes=[blocks, sums],
        compiler_params=params(tiles, history, *received, half, half, blocks, sums),
        name="multiply_tiles",
    )(over, table, size, tiles, history, *received, *after)


def code_kernel(per_owner, where, over, kept, got, own, *coded):
    chunks, part, side = kept.shape
    col = where[1]
    flag = jnp.maximum(over[0].astype(jnp.float32), got[chunks][:1, :LANES])
    for step in list(range(1, chunks // per_owner)) + [0]:
        chunk = lax.bitwise_xor(col, step) * per_owner
        exponents = []
        for block in range(per_owner):
            value = kept[chunk + block] + got[chunk + block]
            if step == 0:
                own[block] = value
                continue
            out = coded[step - 1]
            largest = jnp.maximum(jnp.max(jnp.abs(value), axis=0, keepdims=True), 1e-30)
            exponent = jnp.ceil(jnp.log2(largest))
            grid = jnp.clip(jnp.round(value * jnp.exp2(15.0 - exponent)), -32767.0, 32767.0)
            grid = grid.astype(jnp.int32).astype(jnp.int16)
            for lane in range(side // LANES):
                at = len(exponents)
                out[pl.ds(at * part, part), :] = grid[:, lane * LANES : (lane + 1) * LANES]
                exponents.append(exponent[:, lane * LANES : (lane + 1) * LANES])
        if step > 0:
            at = len(exponents)
            exponents.append(jnp.zeros((PAD - 1 - at, LANES), jnp.float32))
            exponents.append(flag)
            tail = jnp.concatenate(exponents, axis=0)
            out[pl.ds(at * part, PAD), :] = tail.astype(jnp.int32).astype(jnp.int16)


def code(where, over, kept, got, per_owner):
    chunks, part, side = kept.shape
    chunk = jax.ShapeDtypeStruct((per_owner * part * (side // LANES) + PAD, LANES), jnp.int16)
    own = jax.ShapeDtypeStruct((per_owner, part, side), jnp.float32)
    outs = [own] + [chunk] * (chunks // per_owner - 1)
    return pl.pallas_call(
        functools.partial(code_kernel, per_owner),
        out_shape=outs,
        in_specs=[SMEM] * 2 + [VMEM, VMEM],
        out_specs=[VMEM] * len(outs),
        compiler_params=params(kept, got, *outs),
        name="add_and_code",
    )(where, over, kept, got)


def solve_kernel(first, fresh, over, *refs):
    refs = refs if fresh else refs[2:]
    base, rate, direct, state, own = refs[:5]
    codes, (stress_out, rate_out, flag_out, stress_held, rate_held, sems) = refs[5:-6], refs[-6:]
    per_owner, part, side = own.shape
    rows = pl.ds(first, part)
    tails = []
    flag = over[0].astype(jnp.float32)
    for chunk in codes:
        tail = chunk[pl.ds(chunk.shape[0] - PAD, PAD), :].astype(jnp.int32).astype(jnp.float32)
        flag = jnp.maximum(flag, jnp.max(tail[PAD - 1 :, :]))
        tails.append(tail)
    flag_out[0] = flag.astype(jnp.int32)
    for at in range(per_owner * (side // LANES)):
        block, lane = at // (side // LANES), at % (side // LANES)
        stress = own[block, :, pl.ds(lane * LANES, LANES)]
        for chunk, tail in zip(codes, tails):
            values = chunk[pl.ds(at * part, part), :].astype(jnp.int32).astype(jnp.float32)
            stress = stress + values * jnp.exp2(tail[at : at + 1, :] - 15.0)
        lanes = pl.ds(at * LANES, LANES)
        stress_held[:, lanes] = stress
        rate_held[:, lanes] = friction(
            stress, base[rows, lanes], rate[rows, lanes], direct[rows, lanes], state[rows, lanes]
        )
    copies = (
        pltpu.make_async_copy(stress_held, stress_out.at[rows], sems.at[0]),
        pltpu.make_async_copy(rate_held, rate_out.at[rows], sems.at[1]),
    )
    for copy in copies:
        copy.start()
    for copy in copies:
        copy.wait()


def solve(first, over, fields, own, coded, before):
    sims, owned = fields[0].shape
    part = own.shape[1]
    fresh = before is None
    carried = [] if fresh else list(before)
    held = pltpu.VMEM((part, owned), jnp.float32)
    return pl.pallas_call(
        functools.partial(solve_kernel, first, fresh),
        out_shape=[jax.ShapeDtypeStruct(fields[0].shape, jnp.float32)] * 2
        + [jax.ShapeDtypeStruct((1,), jnp.int32)],
        in_specs=[SMEM] + [ANY] * len(carried) + [VMEM] * (5 + len(coded)),
        out_specs=[ANY, ANY, SMEM],
        input_output_aliases={} if fresh else {1: 0, 2: 1},
        scratch_shapes=[held, held, pltpu.SemaphoreType.DMA((2,))],
        compiler_params=params(*fields, own, held, held, *coded),
        name="friction_solve",
    )(over, *carried, *fields, own, *coded)


def reduce(first, where, over, fields, kept, given, before):
    per_owner = fields[0].shape[1] // kept.shape[2]
    col_size = lax.axis_size("col")
    got = lax.ppermute(given, "lag", partners(lax.axis_size("lag"), 1))
    own, *coded = code(where, over, kept, got, per_owner)
    arrived = [None] * (col_size - 1)
    for step in range(col_size - 1, 0, -1):
        arrived[step - 1] = lax.ppermute(coded[step - 1], "col", partners(col_size, step))
    return solve(first, over, fields, own, arrived, before)


def local(history, kernel_tiles, tile_rows, tile_cols, tile_count, base_stress, prev_rate, direct_effect, state_var):
    _, _, lags, slots, side, _ = kernel_tiles.shape
    row_size, col_size = (lax.axis_size(axis) for axis in ("row", "col"))
    where = jnp.stack([lax.axis_index(axis).astype(jnp.int32) for axis in ("row", "col", "lag")])
    history = history[:, 0]
    tiles = kernel_tiles[0, 0]
    sims = history.shape[1]
    cut = sims * FIRST // 8
    pieces = ((0, cut), (cut, sims - cut))
    local_blocks = history.shape[2] // side
    total = row_size * local_blocks
    per_owner = base_stress.shape[1] // side
    chunks = col_size * per_owner
    cap = min(CAP, lags * local_blocks)
    fields = (base_stress, prev_rate, direct_effect, state_var)

    need = make_request(tile_cols, tile_count, total)
    requests = [lax.ppermute(need, "row", partners(row_size, step)) for step in range(1, row_size)]
    held = load(history)
    packed = list(pack(where, requests, held, side, cap, pieces))
    received = [
        [lax.ppermute(packed.pop(0), "row", partners(row_size, step)) for step in range(1, row_size)]
        for _ in pieces
    ]
    table, size, over, live_tiles = make_plan(
        where, tile_cols, tile_rows, tile_count, [need, *requests], tiles, cap, col_size, per_owner
    )

    after = ()
    result = None
    for (first, part), blocks in zip(pieces, received):
        kept, given = multiply_tiles(
            first, part, False, over, table, size, live_tiles, held, blocks, chunks, after
        )
        *result, flag = reduce(first, where, over, fields, kept, given, result)
        after = (flag,)

    def general():
        everything = [lax.ppermute(history, "row", partners(row_size, step)) for step in range(1, row_size)]
        kept, given = multiply_tiles(
            0, sims, True, over, table, size, live_tiles, history, everything, chunks, ()
        )
        return tuple(reduce(0, where, over, fields, kept, given, None)[:2])

    return lax.cond(flag[0] > 0, general, lambda: tuple(result))


def solution(mesh):
    return jax.shard_map(
        local,
        mesh=mesh,
        in_specs=(
            P("lag", "col", None, "row"),
            P("row", "col", "lag", None, None, None),
            P("row", "col", "lag", None),
            P("row", "col", "lag", None),
            P("row", "col", "lag"),
            P(None, ("row", "col", "lag")),
            P(None, ("row", "col", "lag")),
            P(None, ("row", "col", "lag")),
            P(None, ("row", "col", "lag")),
        ),
        out_specs=(P(None, ("row", "col", "lag")), P(None, ("row", "col", "lag"))),
        check_vma=False,
    )
```

```python
import functools
import math

import jax
import jax.numpy as jnp
from jax import lax
from jax.experimental import pallas as pl
from jax.experimental.pallas import tpu as pltpu
from jax.sharding import PartitionSpec as P

NEWTON = 4
CAP = 16
FIRST = 3
PAD = 16
LANES = 128
SPLIT = 2
GROUP = 4
ANY = pl.BlockSpec(memory_space=pl.ANY)
SMEM = pl.BlockSpec(memory_space=pltpu.SMEM)
VMEM = pl.BlockSpec(memory_space=pltpu.VMEM)


def params(*shapes):
    held = sum(math.prod(s.shape) * jnp.dtype(s.dtype).itemsize for s in shapes)
    return pltpu.CompilerParams(vmem_limit_bytes=held + 8 * 1024 * 1024)


def partners(size, step):
    return [(index, index ^ step) for index in range(size)]


def inverse_sinh(value, root):
    length = jnp.log(jnp.abs(value) + root)
    return jnp.where(value < 0.0, -length, length)


def friction(stress, base, velocity, direct, state):
    driving = base + stress
    factor = jnp.exp(state) / 2.0
    gain = direct * factor
    for step in range(NEWTON):
        scaled = velocity * factor
        root = jnp.sqrt(1.0 + scaled * scaled)
        misfit = direct * inverse_sinh(scaled, root) + 0.5 * velocity - driving
        velocity = velocity - misfit / (gain / root + 0.5)
    return velocity


def request_kernel(cols, counts, need):
    lags, total = need.shape
    slots = cols.shape[3]
    names = lax.broadcasted_iota(jnp.int32, (1, total), 1)
    for lag in range(lags):
        marks = jnp.zeros((1, total), jnp.int32)
        for slot in range(slots):
            marks = jnp.where(
                (names == cols[0, 0, lag, slot]) & (slot < counts[0, 0, lag]), 1, marks
            )
        need[lag : lag + 1, :] = marks


def make_request(cols, counts, total):
    return pl.pallas_call(
        request_kernel,
        out_shape=jax.ShapeDtypeStruct((cols.shape[2], total), jnp.int32),
        in_specs=[SMEM, SMEM],
        out_specs=VMEM,
        name="mark_blocks",
    )(cols, counts)


def load_kernel(history, held, sem):
    copy = pltpu.make_async_copy(history, held, sem)
    copy.start()
    copy.wait()


def load(history):
    return pl.pallas_call(
        load_kernel,
        out_shape=history,
        in_specs=[ANY],
        out_specs=VMEM,
        scratch_shapes=[pltpu.SemaphoreType.DMA],
        compiler_params=params(history),
        name="load_history",
    )(history)


def pack_kernel(cap, pieces, side, where, *refs):
    peers = (len(refs) - 1) // (len(pieces) + 1)
    needs, history, packed = refs[:peers], refs[peers], refs[peers + 1 :]
    lags, sims, width = history.shape
    local_blocks = width // side
    first = where[0] * local_blocks
    for peer in range(peers):
        position = jnp.int32(0)
        for lag in range(lags):
            for block in range(local_blocks):
                wanted = needs[peer][lag, first + block]

                @pl.when((wanted > 0) & (position < cap))
                def _(peer=peer, lag=lag, block=block, position=position):
                    for piece, (begin, part) in enumerate(pieces):
                        packed[piece * peers + peer][position] = history[
                            lag, begin : begin + part, block * side : (block + 1) * side
                        ]

                position = position + wanted


def pack(where, needs, history, side, cap, pieces):
    outs = []
    for _, part in pieces:
        outs += [jax.ShapeDtypeStruct((cap, part, side), history.dtype)] * len(needs)
    return pl.pallas_call(
        functools.partial(pack_kernel, cap, pieces, side),
        out_shape=outs,
        in_specs=[SMEM] * (1 + len(needs)) + [VMEM],
        out_specs=[VMEM] * len(outs),
        compiler_params=params(history, *outs),
        name="pack_history",
    )(where, *needs, history)


def plan_kernel(cap, col_size, per_owner, where, cols, rows, counts, *refs):
    needs, tiles, (table, size, over, held, places) = refs[:-6], refs[-6], refs[-5:]
    lags, total = needs[0].shape
    row, core = where[0], where[2]
    members = len(needs)
    local_blocks = total // members
    for owner in range(members):
        position = jnp.int32(0)
        for lag in range(lags):
            for block in range(owner * local_blocks, (owner + 1) * local_blocks):
                places[lag, block] = position
                position = position + needs[0][lag, block]
    above = jnp.int32(0)
    for member in range(members):
        for owner in range(members):
            wanted = jnp.int32(0)
            for lag in range(lags):
                for block in range(local_blocks):
                    wanted = wanted + needs[member][lag, owner * local_blocks + block]
            foreign = lax.bitwise_xor(row, member) != owner
            above = jnp.where(foreign & (wanted > cap), 1, above)
    over[0] = above
    filled = jnp.int32(0)
    for lag in range(lags):

        def note(slot, filled, lag=lag):
            col = cols[0, 0, lag, slot]
            target = rows[0, 0, lag, slot]
            owner = target // per_owner
            half = lax.bitwise_xor(owner % 2, core) * col_size + owner // 2
            table[0, filled] = lag
            table[1, filled] = lax.bitwise_xor(col // local_blocks, row)
            table[2, filled] = col % local_blocks
            table[3, filled] = jnp.minimum(places[lag, col], cap - 1)
            table[4, filled] = half * per_owner + target % per_owner
            held[filled] = tiles[lag, slot]
            return filled + 1

        filled = lax.fori_loop(0, counts[0, 0, lag], note, filled)
    size[0] = filled


def make_plan(where, cols, rows, counts, needs, tiles, cap, col_size, per_owner):
    lags, total = needs[0].shape
    count = lags * cols.shape[3]
    held = jax.ShapeDtypeStruct((count,) + tiles.shape[2:], tiles.dtype)
    return pl.pallas_call(
        functools.partial(plan_kernel, cap, col_size, per_owner),
        out_shape=[
            jax.ShapeDtypeStruct((5, count), jnp.int32),
            jax.ShapeDtypeStruct((1,), jnp.int32),
            jax.ShapeDtypeStruct((1,), jnp.int32),
            held,
        ],
        in_specs=[SMEM] * (4 + len(needs)) + [VMEM],
        out_specs=[SMEM] * 3 + [VMEM],
        scratch_shapes=[pltpu.SMEM((lags, total), jnp.int32)],
        compiler_params=params(tiles, held),
        name="plan_tiles",
    )(where, cols, rows, counts, *needs, tiles)


def tiles_kernel(first, whole, extra, over, table, size, tiles, history, *refs):
    received, given = refs[: len(refs) - 3 - SPLIT - extra], refs[-2 - SPLIT : -2]
    kept, (blocks, sums) = refs[-3 - SPLIT], refs[-2:]
    side = tiles.shape[2]
    halves, part, _ = sums.shape
    live = size[0]
    sums[...] = jnp.zeros_like(sums)

    def fetch(index, carry):
        lag, relative = table[0, index], table[1, index]
        lanes = pl.ds(pl.multiple_of(table[2, index] * side, side), side)

        @pl.when(relative == 0)
        def _():
            blocks[index] = history[lag, pl.ds(first, part), lanes]

        for peer in range(len(received)):

            @pl.when(relative == peer + 1)
            def _(peer=peer):
                if whole:
                    blocks[index] = received[peer][lag, pl.ds(first, part), lanes]
                else:
                    blocks[index] = received[peer][table[3, index]]

        return carry

    lax.fori_loop(0, live, fetch, 0)

    def multiply(group, carry):
        products = []
        for offset in range(GROUP):
            index = jnp.minimum(group * GROUP + offset, live - 1)
            products.append(
                lax.dot_general(
                    blocks[index], tiles[index], (((1,), (1,)), ((), ())), preferred_element_type=jnp.float32
                )
            )
        for offset, product in enumerate(products):
            index = group * GROUP + offset
            spot = table[4, jnp.minimum(index, live - 1)]
            sums[spot] += product if offset == 0 else jnp.where(index < live, product, 0.0)
        return carry

    lax.fori_loop(0, (live + GROUP - 1) // GROUP, multiply, 0)
    kept[...] = sums[: halves // 2]
    half = halves // 2
    for index, target in enumerate(given):
        size = half // SPLIT
        target[:size] = sums[half + index * size : half + (index + 1) * size]
    given[0][half // SPLIT] = jnp.full((part, side), 1.0, jnp.float32) * over[0].astype(jnp.float32)


def multiply_tiles(first, part, whole, over, table, size, tiles, history, received, chunks, after):
    side = tiles.shape[2]
    half = jax.ShapeDtypeStruct((chunks, part, side), jnp.float32)
    more = [
        jax.ShapeDtypeStruct((chunks // SPLIT + (index == 0), part, side), jnp.float32) for index in range(SPLIT)
    ]
    blocks = pltpu.VMEM((table.shape[1], part, side), history.dtype)
    sums = pltpu.VMEM((2 * chunks, part, side), jnp.float32)
    return pl.pallas_call(
        functools.partial(tiles_kernel, first, whole, len(after)),
        out_shape=[half, *more],
        in_specs=[SMEM] * 3 + [VMEM] * (2 + len(received)) + [ANY] * len(after),
        out_specs=[VMEM] * (1 + SPLIT),
        scratch_shapes=[blocks, sums],
        compiler_params=params(tiles, history, *received, half, half, blocks, sums),
        name="multiply_tiles",
    )(over, table, size, tiles, history, *received, *after)


def code_kernel(per_owner, where, over, kept, *refs):
    got, own, coded, theirs = refs[:SPLIT], refs[SPLIT], refs[SPLIT + 1 : -1], refs[-1]
    chunks, part, side = kept.shape
    size = chunks // SPLIT
    for index, source in enumerate(got):
        theirs[index * size : (index + 1) * size] = source[:size]
    col = where[1]
    flag = jnp.maximum(over[0].astype(jnp.float32), got[0][size][:1, :LANES])
    for step in list(range(1, chunks // per_owner)) + [0]:
        chunk = lax.bitwise_xor(col, step) * per_owner
        exponents = []
        for block in range(per_owner):
            value = kept[chunk + block] + theirs[chunk + block]
            if step == 0:
                own[block] = value
                continue
            out = coded[step - 1]
            largest = jnp.maximum(jnp.max(jnp.abs(value), axis=0, keepdims=True), 1e-30)
            exponent = jnp.ceil(jnp.log2(largest))
            grid = jnp.clip(jnp.round(value * jnp.exp2(15.0 - exponent)), -32767.0, 32767.0)
            grid = grid.astype(jnp.int32).astype(jnp.int16)
            for lane in range(side // LANES):
                at = len(exponents)
                out[pl.ds(at * part, part), :] = grid[:, lane * LANES : (lane + 1) * LANES]
                exponents.append(exponent[:, lane * LANES : (lane + 1) * LANES])
        if step > 0:
            at = len(exponents)
            exponents.append(jnp.zeros((PAD - 1 - at, LANES), jnp.float32))
            exponents.append(flag)
            tail = jnp.concatenate(exponents, axis=0)
            out[pl.ds(at * part, PAD), :] = tail.astype(jnp.int32).astype(jnp.int16)


def code(where, over, kept, got, per_owner):
    chunks, part, side = kept.shape
    chunk = jax.ShapeDtypeStruct((per_owner * part * (side // LANES) + PAD, LANES), jnp.int16)
    own = jax.ShapeDtypeStruct((per_owner, part, side), jnp.float32)
    outs = [own] + [chunk] * (chunks // per_owner - 1)
    return pl.pallas_call(
        functools.partial(code_kernel, per_owner),
        out_shape=outs,
        in_specs=[SMEM] * 2 + [VMEM] * (1 + len(got)),
        out_specs=[VMEM] * len(outs),
        scratch_shapes=[pltpu.VMEM(kept.shape, jnp.float32)],
        compiler_params=params(kept, kept, *got, *outs),
        name="add_and_code",
    )(where, over, kept, *got)


def solve_kernel(first, fresh, over, *refs):
    refs = refs if fresh else refs[2:]
    base, rate, direct, state, own = refs[:5]
    codes, (stress_out, rate_out, flag_out, stress_held, rate_held, sems) = refs[5:-6], refs[-6:]
    per_owner, part, side = own.shape
    rows = pl.ds(first, part)
    tails = []
    flag = over[0].astype(jnp.float32)
    for chunk in codes:
        tail = chunk[pl.ds(chunk.shape[0] - PAD, PAD), :].astype(jnp.int32).astype(jnp.float32)
        flag = jnp.maximum(flag, jnp.max(tail[PAD - 1 :, :]))
        tails.append(tail)
    flag_out[0] = flag.astype(jnp.int32)
    for at in range(per_owner * (side // LANES)):
        block, lane = at // (side // LANES), at % (side // LANES)
        stress = own[block, :, pl.ds(lane * LANES, LANES)]
        for chunk, tail in zip(codes, tails):
            values = chunk[pl.ds(at * part, part), :].astype(jnp.int32).astype(jnp.float32)
            stress = stress + values * jnp.exp2(tail[at : at + 1, :] - 15.0)
        lanes = pl.ds(at * LANES, LANES)
        stress_held[:, lanes] = stress
        rate_held[:, lanes] = friction(
            stress, base[rows, lanes], rate[rows, lanes], direct[rows, lanes], state[rows, lanes]
        )
    copies = (
        pltpu.make_async_copy(stress_held, stress_out.at[rows], sems.at[0]),
        pltpu.make_async_copy(rate_held, rate_out.at[rows], sems.at[1]),
    )
    for copy in copies:
        copy.start()
    for copy in copies:
        copy.wait()


def solve(first, over, fields, own, coded, before):
    sims, owned = fields[0].shape
    part = own.shape[1]
    fresh = before is None
    carried = [] if fresh else list(before)
    held = pltpu.VMEM((part, owned), jnp.float32)
    return pl.pallas_call(
        functools.partial(solve_kernel, first, fresh),
        out_shape=[jax.ShapeDtypeStruct(fields[0].shape, jnp.float32)] * 2
        + [jax.ShapeDtypeStruct((1,), jnp.int32)],
        in_specs=[SMEM] + [ANY] * len(carried) + [VMEM] * (5 + len(coded)),
        out_specs=[ANY, ANY, SMEM],
        input_output_aliases={} if fresh else {1: 0, 2: 1},
        scratch_shapes=[held, held, pltpu.SemaphoreType.DMA((2,))],
        compiler_params=params(*fields, own, held, held, *coded),
        name="friction_solve",
    )(over, *carried, *fields, own, *coded)


def reduce(first, where, over, fields, kept, given, before):
    per_owner = fields[0].shape[1] // kept.shape[2]
    col_size = lax.axis_size("col")
    got = [lax.ppermute(array, "lag", partners(lax.axis_size("lag"), 1)) for array in given]
    own, *coded = code(where, over, kept, got, per_owner)
    arrived = [None] * (col_size - 1)
    for step in range(col_size - 1, 0, -1):
        arrived[step - 1] = lax.ppermute(coded[step - 1], "col", partners(col_size, step))
    return solve(first, over, fields, own, arrived, before)


def local(history, kernel_tiles, tile_rows, tile_cols, tile_count, base_stress, prev_rate, direct_effect, state_var):
    _, _, lags, slots, side, _ = kernel_tiles.shape
    row_size, col_size = (lax.axis_size(axis) for axis in ("row", "col"))
    where = jnp.stack([lax.axis_index(axis).astype(jnp.int32) for axis in ("row", "col", "lag")])
    history = history[:, 0]
    tiles = kernel_tiles[0, 0]
    sims = history.shape[1]
    cut = sims * FIRST // 8
    pieces = ((0, cut), (cut, sims - cut))
    local_blocks = history.shape[2] // side
    total = row_size * local_blocks
    per_owner = base_stress.shape[1] // side
    chunks = col_size * per_owner
    cap = min(CAP, lags * local_blocks)
    fields = (base_stress, prev_rate, direct_effect, state_var)

    need = make_request(tile_cols, tile_count, total)
    requests = [lax.ppermute(need, "row", partners(row_size, step)) for step in range(1, row_size)]
    held = load(history)
    packed = list(pack(where, requests, held, side, cap, pieces))
    received = [
        [lax.ppermute(packed.pop(0), "row", partners(row_size, step)) for step in range(1, row_size)]
        for _ in pieces
    ]
    table, size, over, live_tiles = make_plan(
        where, tile_cols, tile_rows, tile_count, [need, *requests], tiles, cap, col_size, per_owner
    )

    after = ()
    result = None
    for (first, part), blocks in zip(pieces, received):
        kept, *given = multiply_tiles(
            first, part, False, over, table, size, live_tiles, held, blocks, chunks, after
        )
        *result, flag = reduce(first, where, over, fields, kept, given, result)
        after = (flag,)

    def general():
        everything = [lax.ppermute(history, "row", partners(row_size, step)) for step in range(1, row_size)]
        kept, *given = multiply_tiles(
            0, sims, True, over, table, size, live_tiles, history, everything, chunks, ()
        )
        return tuple(reduce(0, where, over, fields, kept, given, None)[:2])

    return lax.cond(flag[0] > 0, general, lambda: tuple(result))


def solution(mesh):
    return jax.shard_map(
        local,
        mesh=mesh,
        in_specs=(
            P("lag", "col", None, "row"),
            P("row", "col", "lag", None, None, None),
            P("row", "col", "lag", None),
            P("row", "col", "lag", None),
            P("row", "col", "lag"),
            P(None, ("row", "col", "lag")),
            P(None, ("row", "col", "lag")),
            P(None, ("row", "col", "lag")),
            P(None, ("row", "col", "lag")),
        ),
        out_specs=(P(None, ("row", "col", "lag")), P(None, ("row", "col", "lag"))),
        check_vma=False,
    )
```

```python
import functools
import math

import jax
import jax.numpy as jnp
from jax import lax
from jax.experimental import pallas as pl
from jax.experimental.pallas import tpu as pltpu
from jax.sharding import PartitionSpec as P

NEWTON = 4
CAP = 16
PIECES = (4, 4)
PAD = 16
LANES = 128
SPLIT = 2
WAIT = 1
GROUP = 8
ANY = pl.BlockSpec(memory_space=pl.ANY)
SMEM = pl.BlockSpec(memory_space=pltpu.SMEM)
VMEM = pl.BlockSpec(memory_space=pltpu.VMEM)


def params(*shapes):
    held = sum(math.prod(s.shape) * jnp.dtype(s.dtype).itemsize for s in shapes)
    return pltpu.CompilerParams(vmem_limit_bytes=held + 8 * 1024 * 1024)


def partners(size, step):
    return [(index, index ^ step) for index in range(size)]


def friction(stress, base, velocity, direct, state):
    driving = base + stress
    factor = jnp.exp(state) / 2.0
    gain = direct * factor
    for step in range(NEWTON):
        scaled = velocity * factor
        square = 1.0 + scaled * scaled
        inverse = lax.rsqrt(square)
        length = jnp.log(jnp.abs(scaled) + square * inverse)
        misfit = direct * jnp.where(scaled < 0.0, -length, length) + 0.5 * velocity - driving
        velocity = velocity - misfit / (gain * inverse + 0.5)
    return velocity


def request_kernel(cols, counts, need):
    lags, total = need.shape
    slots = cols.shape[3]
    names = lax.broadcasted_iota(jnp.int32, (1, total), 1)
    for lag in range(lags):
        marks = jnp.zeros((1, total), jnp.int32)
        for slot in range(slots):
            marks = jnp.where(
                (names == cols[0, 0, lag, slot]) & (slot < counts[0, 0, lag]), 1, marks
            )
        need[lag : lag + 1, :] = marks


def make_request(cols, counts, total):
    return pl.pallas_call(
        request_kernel,
        out_shape=jax.ShapeDtypeStruct((cols.shape[2], total), jnp.int32),
        in_specs=[SMEM, SMEM],
        out_specs=VMEM,
        name="mark_blocks",
    )(cols, counts)


def load_kernel(history, held, sem):
    copy = pltpu.make_async_copy(history, held, sem)
    copy.start()
    copy.wait()


def load(history):
    return pl.pallas_call(
        load_kernel,
        out_shape=history,
        in_specs=[ANY],
        out_specs=VMEM,
        scratch_shapes=[pltpu.SemaphoreType.DMA],
        compiler_params=params(history),
        name="load_history",
    )(history)


def pack_kernel(cap, piece, side, extra, where, *refs):
    begin, part = piece
    peers = (len(refs) - 1 - extra) // 2
    needs, history, packed = refs[:peers], refs[peers], refs[peers + 1 + extra :]
    lags, sims, width = history.shape
    local_blocks = width // side
    first = where[0] * local_blocks
    for peer in range(peers):
        position = jnp.int32(0)
        for lag in range(lags):
            for block in range(local_blocks):
                wanted = needs[peer][lag, first + block]

                @pl.when((wanted > 0) & (position < cap))
                def _(peer=peer, lag=lag, block=block, position=position):
                    packed[peer][position] = history[
                        lag, begin : begin + part, block * side : (block + 1) * side
                    ]

                position = position + wanted


def pack(where, needs, history, side, cap, piece, after):
    outs = [jax.ShapeDtypeStruct((cap, piece[1], side), history.dtype)] * len(needs)
    return pl.pallas_call(
        functools.partial(pack_kernel, cap, piece, side, len(after)),
        out_shape=outs,
        in_specs=[SMEM] * (1 + len(needs)) + [VMEM] + [ANY] * len(after),
        out_specs=[VMEM] * len(outs),
        compiler_params=params(history, *outs),
        name="pack_history",
    )(where, *needs, history, *after)


def plan_kernel(cap, col_size, per_owner, where, cols, rows, counts, *refs):
    needs, tiles, (table, size, over, held, places, ends) = refs[:-7], refs[-7], refs[-6:]
    lags, total = needs[0].shape
    row, core = where[0], where[2]
    members = len(needs)
    local_blocks = total // members
    for owner in range(members):
        position = jnp.int32(0)
        for lag in range(lags):
            for block in range(owner * local_blocks, (owner + 1) * local_blocks):
                places[lag, block] = position
                position = position + needs[0][lag, block]
    above = jnp.int32(0)
    for member in range(members):
        for owner in range(members):
            wanted = jnp.int32(0)
            for lag in range(lags):
                for block in range(local_blocks):
                    wanted = wanted + needs[member][lag, owner * local_blocks + block]
            foreign = lax.bitwise_xor(row, member) != owner
            above = jnp.where(foreign & (wanted > cap), 1, above)
    over[0] = above
    tally = [jnp.int32(0)] * members
    for lag in range(lags):

        def tell(slot, tally, lag=lag):
            source = lax.bitwise_xor(cols[0, 0, lag, slot] // local_blocks, row)
            return tuple(count + (source == index).astype(jnp.int32) for index, count in enumerate(tally))

        tally = lax.fori_loop(0, counts[0, 0, lag], tell, tuple(tally))
    begin = jnp.int32(0)
    for member in range(members):
        size[member] = begin
        ends[member] = begin
        begin = begin + tally[member]
    size[members] = begin
    for lag in range(lags):

        def note(slot, carry, lag=lag):
            col = cols[0, 0, lag, slot]
            target = rows[0, 0, lag, slot]
            owner = target // per_owner
            half = lax.bitwise_xor(owner % 2, core) * col_size + owner // 2
            source = lax.bitwise_xor(col // local_blocks, row)
            filled = ends[source]
            ends[source] = filled + 1
            table[0, filled] = lag
            table[1, filled] = half * per_owner + target % per_owner
            table[2, filled] = col % local_blocks
            table[3, filled] = jnp.minimum(places[lag, col], cap - 1)
            held[filled] = tiles[lag, slot]
            return carry

        lax.fori_loop(0, counts[0, 0, lag], note, 0)


def make_plan(where, cols, rows, counts, needs, tiles, cap, col_size, per_owner):
    lags, total = needs[0].shape
    count = lags * cols.shape[3]
    held = jax.ShapeDtypeStruct((count,) + tiles.shape[2:], tiles.dtype)
    return pl.pallas_call(
        functools.partial(plan_kernel, cap, col_size, per_owner),
        out_shape=[
            jax.ShapeDtypeStruct((4, count), jnp.int32),
            jax.ShapeDtypeStruct((len(needs) + 1,), jnp.int32),
            jax.ShapeDtypeStruct((1,), jnp.int32),
            held,
        ],
        in_specs=[SMEM] * (4 + len(needs)) + [VMEM],
        out_specs=[SMEM] * 3 + [VMEM],
        scratch_shapes=[pltpu.SMEM((lags, total), jnp.int32), pltpu.SMEM((len(needs),), jnp.int32)],
        compiler_params=params(tiles, held),
        name="plan_tiles",
    )(where, cols, rows, counts, *needs, tiles)


def tiles_kernel(first, whole, extra, over, table, size, tiles, history, *refs):
    received, (sums, *given), blocks = refs[: len(refs) - 2 - SPLIT - extra], refs[-2 - SPLIT : -1], refs[-1]
    side = tiles.shape[2]
    halves, part, _ = sums.shape
    live = size[len(received) + 1]
    sums[...] = jnp.zeros_like(sums)

    def fetch(source):
        def one(index, carry):
            lanes = pl.ds(pl.multiple_of(table[2, index] * side, side), side)
            if source == 0:
                blocks[index] = history[table[0, index], pl.ds(first, part), lanes]
            elif whole:
                blocks[index] = received[source - 1][table[0, index], pl.ds(first, part), lanes]
            else:
                blocks[index] = received[source - 1][table[3, index]]
            return carry

        return one

    for source in range(len(received) + 1):
        lax.fori_loop(size[source], size[source + 1], fetch(source), 0)

    def multiply(group, carry):
        products = []
        for offset in range(GROUP):
            index = jnp.minimum(group * GROUP + offset, live - 1)
            products.append(
                lax.dot_general(
                    blocks[index], tiles[index], (((1,), (1,)), ((), ())), preferred_element_type=jnp.float32
                )
            )
        for offset, product in enumerate(products):
            index = group * GROUP + offset
            spot = table[1, jnp.minimum(index, live - 1)]
            sums[spot] += product if offset == 0 else jnp.where(index < live, product, 0.0)
        return carry

    lax.fori_loop(0, (live + GROUP - 1) // GROUP, multiply, 0)
    half = halves // 2
    size = half // SPLIT
    flag = jnp.full((1, side), 1.0, jnp.float32) * over[0].astype(jnp.float32)
    for index, target in enumerate(given):
        exponents = []
        for chunk in range(size):
            grid, exponent = to_fixed(sums[half + index * size + chunk])
            target[chunk * part : (chunk + 1) * part] = grid
            exponents.append(exponent)
        exponents += [jnp.zeros((PAD - 1 - size, side), jnp.float32), flag]
        tail = jnp.concatenate(exponents, axis=0)
        target[size * part :] = tail.astype(jnp.int32).astype(jnp.int16)


def multiply_tiles(first, part, whole, over, table, size, tiles, history, received, chunks, after):
    side = tiles.shape[2]
    more = [jax.ShapeDtypeStruct((chunks // SPLIT * part + PAD, side), jnp.int16)] * SPLIT
    blocks = pltpu.VMEM((table.shape[1], part, side), history.dtype)
    sums = jax.ShapeDtypeStruct((2 * chunks, part, side), jnp.float32)
    return pl.pallas_call(
        functools.partial(tiles_kernel, first, whole, len(after)),
        out_shape=[sums, *more],
        in_specs=[SMEM] * 3 + [VMEM] * (2 + len(received)) + [ANY] * len(after),
        out_specs=[VMEM] * (1 + SPLIT),
        scratch_shapes=[blocks],
        compiler_params=params(tiles, history, *received, *more, blocks, sums),
        name="multiply_tiles",
    )(over, table, size, tiles, history, *received, *after)


def to_fixed(value):
    largest = jnp.maximum(jnp.max(jnp.abs(value), axis=0, keepdims=True), 1e-30)
    exponent = jnp.ceil(jnp.log2(largest))
    grid = jnp.clip(jnp.round(value * jnp.exp2(15.0 - exponent)), -32767.0, 32767.0)
    return grid.astype(jnp.int32).astype(jnp.int16), exponent


def from_fixed(grid, exponent):
    return grid.astype(jnp.int32).astype(jnp.float32) * jnp.exp2(exponent - 15.0)


def code_kernel(per_owner, extra, where, over, kept, *refs):
    got, own, coded = refs[:SPLIT], refs[SPLIT + extra], refs[SPLIT + extra + 1 : -1]
    theirs = refs[-1]
    chunks, part, side = theirs.shape
    size = chunks // SPLIT
    flag = over[0].astype(jnp.float32)
    for index, source in enumerate(got):
        tail = source[size * part :, :].astype(jnp.int32).astype(jnp.float32)
        flag = jnp.maximum(flag, tail[PAD - 1 :, :LANES])
        for chunk in range(size):
            theirs[index * size + chunk] = from_fixed(
                source[chunk * part : (chunk + 1) * part, :], tail[chunk : chunk + 1, :]
            )
    col = where[1]
    for step in list(range(1, chunks // per_owner)) + [0]:
        chunk = lax.bitwise_xor(col, step) * per_owner
        exponents = []
        for block in range(per_owner):
            value = kept[chunk + block] + theirs[chunk + block]
            if step == 0:
                own[block] = value
                continue
            out = coded[step - 1]
            grid, exponent = to_fixed(value)
            for lane in range(side // LANES):
                at = len(exponents)
                out[pl.ds(at * part, part), :] = grid[:, lane * LANES : (lane + 1) * LANES]
                exponents.append(exponent[:, lane * LANES : (lane + 1) * LANES])
        if step > 0:
            at = len(exponents)
            exponents.append(jnp.zeros((PAD - 1 - at, LANES), jnp.float32))
            exponents.append(flag)
            tail = jnp.concatenate(exponents, axis=0)
            out[pl.ds(at * part, PAD), :] = tail.astype(jnp.int32).astype(jnp.int16)


def code(where, over, kept, got, per_owner, after):
    chunks, part, side = kept.shape
    chunks = chunks // 2
    chunk = jax.ShapeDtypeStruct((per_owner * part * (side // LANES) + PAD, LANES), jnp.int16)
    own = jax.ShapeDtypeStruct((per_owner, part, side), jnp.float32)
    outs = [own] + [chunk] * (chunks // per_owner - 1)
    return pl.pallas_call(
        functools.partial(code_kernel, per_owner, len(after)),
        out_shape=outs,
        in_specs=[SMEM] * 2 + [VMEM] * (1 + len(got)) + [ANY] * len(after),
        out_specs=[VMEM] * len(outs),
        scratch_shapes=[pltpu.VMEM((chunks, part, side), jnp.float32)],
        compiler_params=params(kept, kept, *got, *outs),
        name="add_and_code",
    )(where, over, kept, *got, *after)


def solve_kernel(first, fresh, over, *refs):
    refs = refs if fresh else refs[2:]
    base, rate, direct, state, own = refs[:5]
    codes, (stress_out, rate_out, flag_out, stress_held, rate_held, sems) = refs[5:-6], refs[-6:]
    per_owner, part, side = own.shape
    rows = pl.ds(first, part)
    tails = []
    flag = over[0].astype(jnp.float32)
    for chunk in codes:
        tail = chunk[pl.ds(chunk.shape[0] - PAD, PAD), :].astype(jnp.int32).astype(jnp.float32)
        flag = jnp.maximum(flag, jnp.max(tail[PAD - 1 :, :]))
        tails.append(tail)
    flag_out[0] = flag.astype(jnp.int32)
    for at in range(per_owner * (side // LANES)):
        block, lane = at // (side // LANES), at % (side // LANES)
        stress = own[block, :, pl.ds(lane * LANES, LANES)]
        for chunk, tail in zip(codes, tails):
            stress = stress + from_fixed(chunk[pl.ds(at * part, part), :], tail[at : at + 1, :])
        lanes = pl.ds(at * LANES, LANES)
        stress_held[:, lanes] = stress
        rate_held[:, lanes] = friction(
            stress, base[rows, lanes], rate[rows, lanes], direct[rows, lanes], state[rows, lanes]
        )
    copies = (
        pltpu.make_async_copy(stress_held, stress_out.at[rows], sems.at[0]),
        pltpu.make_async_copy(rate_held, rate_out.at[rows], sems.at[1]),
    )
    for copy in copies:
        copy.start()
    for copy in copies:
        copy.wait()


def solve(first, over, fields, own, coded, before):
    sims, owned = fields[0].shape
    part = own.shape[1]
    fresh = before is None
    carried = [] if fresh else list(before)
    held = pltpu.VMEM((part, owned), jnp.float32)
    return pl.pallas_call(
        functools.partial(solve_kernel, first, fresh),
        out_shape=[jax.ShapeDtypeStruct(fields[0].shape, jnp.float32)] * 2
        + [jax.ShapeDtypeStruct((1,), jnp.int32)],
        in_specs=[SMEM] + [ANY] * len(carried) + [VMEM] * (5 + len(coded)),
        out_specs=[ANY, ANY, SMEM],
        input_output_aliases={} if fresh else {1: 0, 2: 1},
        scratch_shapes=[held, held, pltpu.SemaphoreType.DMA((2,))],
        compiler_params=params(*fields, own, held, held, *coded),
        name="friction_solve",
    )(over, *carried, *fields, own, *coded)


def reduce(first, where, over, fields, kept, given, before, after):
    per_owner = fields[0].shape[1] // kept.shape[2]
    col_size = lax.axis_size("col")
    got = [lax.ppermute(array, "lag", partners(lax.axis_size("lag"), 1)) for array in given]
    own, *coded = code(where, over, kept, got, per_owner, after)
    arrived = [
        lax.ppermute(coded[step - 1], "col", partners(col_size, step)) for step in [*range(2, col_size), 1]
    ]
    return solve(first, over, fields, own, arrived, before), (arrived[0], arrived[1]), tuple(arrived)


def local(history, kernel_tiles, tile_rows, tile_cols, tile_count, base_stress, prev_rate, direct_effect, state_var):
    _, _, lags, slots, side, _ = kernel_tiles.shape
    row_size, col_size = (lax.axis_size(axis) for axis in ("row", "col"))
    where = jnp.stack([lax.axis_index(axis).astype(jnp.int32) for axis in ("row", "col", "lag")])
    history = history[:, 0]
    tiles = kernel_tiles[0, 0]
    sims = history.shape[1]
    pieces = []
    for eighths in PIECES:
        pieces.append((sum(part for _, part in pieces), sims * eighths // 8))
    local_blocks = history.shape[2] // side
    total = row_size * local_blocks
    per_owner = base_stress.shape[1] // side
    chunks = col_size * per_owner
    cap = min(CAP, lags * local_blocks)
    fields = (base_stress, prev_rate, direct_effect, state_var)

    need = make_request(tile_cols, tile_count, total)
    requests = [lax.ppermute(need, "row", partners(row_size, step)) for step in range(1, row_size)]
    held = load(history)
    received = []
    for piece in pieces:
        packed = pack(where, requests, held, side, cap, piece, received[-1][:WAIT] if received else ())
        received.append(
            [lax.ppermute(packed[step - 1], "row", partners(row_size, step)) for step in range(1, row_size)]
        )
    table, size, over, live_tiles = make_plan(
        where, tile_cols, tile_rows, tile_count, [need, *requests], tiles, cap, col_size, per_owner
    )

    after = ()
    result = None
    for (first, part), blocks in zip(pieces, received):
        kept, *given = multiply_tiles(
            first, part, False, over, table, size, live_tiles, held, blocks, chunks, after
        )
        (*result, flag), after, _ = reduce(first, where, over, fields, kept, given, result, ())

    def general():
        everything = [lax.ppermute(history, "row", partners(row_size, step)) for step in range(1, row_size)]
        kept, *given = multiply_tiles(
            0, sims, True, over, table, size, live_tiles, history, everything, chunks, ()
        )
        return tuple(reduce(0, where, over, fields, kept, given, None, ())[0][:2])

    return lax.cond(flag[0] > 0, general, lambda: tuple(result))


def solution(mesh):
    return jax.shard_map(
        local,
        mesh=mesh,
        in_specs=(
            P("lag", "col", None, "row"),
            P("row", "col", "lag", None, None, None),
            P("row", "col", "lag", None),
            P("row", "col", "lag", None),
            P("row", "col", "lag"),
            P(None, ("row", "col", "lag")),
            P(None, ("row", "col", "lag")),
            P(None, ("row", "col", "lag")),
            P(None, ("row", "col", "lag")),
        ),
        out_specs=(P(None, ("row", "col", "lag")), P(None, ("row", "col", "lag"))),
        check_vma=False,
    )
```

```python
import functools
import math

import jax
import jax.numpy as jnp
from jax import lax
from jax.experimental import pallas as pl
from jax.experimental.pallas import tpu as pltpu
from jax.sharding import PartitionSpec as P

NEWTON = 4
CAP = 16
PIECES = (4, 4)
PAD = 16
LANES = 128
OVER = 16
SPLIT = 2
WAIT = 1
GROUP = 8
ANY = pl.BlockSpec(memory_space=pl.ANY)
SMEM = pl.BlockSpec(memory_space=pltpu.SMEM)
VMEM = pl.BlockSpec(memory_space=pltpu.VMEM)


def params(*shapes):
    held = sum(math.prod(s.shape) * jnp.dtype(s.dtype).itemsize for s in shapes)
    return pltpu.CompilerParams(vmem_limit_bytes=held + 8 * 1024 * 1024)


def partners(size, step):
    return [(index, index ^ step) for index in range(size)]


def friction(stress, base, velocity, direct, state):
    driving = base + stress
    factor = jnp.exp(state) / 2.0
    gain = direct * factor
    for step in range(NEWTON):
        scaled = velocity * factor
        square = 1.0 + scaled * scaled
        inverse = lax.rsqrt(square)
        length = jnp.log(jnp.abs(scaled) + square * inverse)
        misfit = direct * jnp.where(scaled < 0.0, -length, length) + 0.5 * velocity - driving
        velocity = velocity - misfit / (gain * inverse + 0.5)
    return velocity


def request_kernel(cols, counts, need):
    lags, total = need.shape
    slots = cols.shape[3]
    names = lax.broadcasted_iota(jnp.int32, (1, total), 1)
    for lag in range(lags):
        marks = jnp.zeros((1, total), jnp.int32)
        for slot in range(slots):
            marks = jnp.where(
                (names == cols[0, 0, lag, slot]) & (slot < counts[0, 0, lag]), 1, marks
            )
        need[lag : lag + 1, :] = marks


def make_request(cols, counts, total):
    return pl.pallas_call(
        request_kernel,
        out_shape=jax.ShapeDtypeStruct((cols.shape[2], total), jnp.int32),
        in_specs=[SMEM, SMEM],
        out_specs=VMEM,
        name="mark_blocks",
    )(cols, counts)


def load_kernel(history, held, sem):
    copy = pltpu.make_async_copy(history, held, sem)
    copy.start()
    copy.wait()


def load(history):
    return pl.pallas_call(
        load_kernel,
        out_shape=history,
        in_specs=[ANY],
        out_specs=VMEM,
        scratch_shapes=[pltpu.SemaphoreType.DMA],
        compiler_params=params(history),
        name="load_history",
    )(history)


def pack_kernel(cap, piece, side, extra, *refs):
    begin, part = piece
    peers = (len(refs) - 1 - extra) // 2
    needs, history, packed = refs[:peers], refs[peers], refs[peers + 1 + extra :]
    lags, sims, width = history.shape
    local_blocks = width // side
    first = lax.axis_index("row") * local_blocks
    for peer in range(peers):
        position = jnp.int32(0)
        for lag in range(lags):
            for block in range(local_blocks):
                wanted = needs[peer][lag, first + block]

                @pl.when((wanted > 0) & (position < cap))
                def _(peer=peer, lag=lag, block=block, position=position):
                    packed[peer][position] = history[
                        lag, begin : begin + part, block * side : (block + 1) * side
                    ]

                position = position + wanted


def pack(needs, history, side, cap, piece, after):
    outs = [jax.ShapeDtypeStruct((cap, piece[1], side), history.dtype)] * len(needs)
    return pl.pallas_call(
        functools.partial(pack_kernel, cap, piece, side, len(after)),
        out_shape=outs,
        in_specs=[SMEM] * len(needs) + [VMEM] + [ANY] * len(after),
        out_specs=[VMEM] * len(outs),
        compiler_params=params(history, *outs),
        name="pack_history",
    )(*needs, history, *after)


def plan_kernel(cap, col_size, per_owner, cols, rows, counts, *refs):
    needs, tiles, (table, held, places, ends) = refs[:-5], refs[-5], refs[-4:]
    lags, total = needs[0].shape
    row, core = lax.axis_index("row"), lax.axis_index("lag")
    members = len(needs)
    local_blocks = total // members
    for owner in range(members):
        position = jnp.int32(0)
        for lag in range(lags):
            for block in range(owner * local_blocks, (owner + 1) * local_blocks):
                places[lag, block] = position
                position = position + needs[0][lag, block]
    above = jnp.int32(0)
    for member in range(members):
        for owner in range(members):
            wanted = jnp.int32(0)
            for lag in range(lags):
                for block in range(local_blocks):
                    wanted = wanted + needs[member][lag, owner * local_blocks + block]
            foreign = lax.bitwise_xor(row, member) != owner
            above = jnp.where(foreign & (wanted > cap), 1, above)
    table[4, OVER] = above
    tally = [jnp.int32(0)] * members
    for lag in range(lags):

        def tell(slot, tally, lag=lag):
            source = lax.bitwise_xor(cols[0, 0, lag, slot] // local_blocks, row)
            return tuple(count + (source == index).astype(jnp.int32) for index, count in enumerate(tally))

        tally = lax.fori_loop(0, counts[0, 0, lag], tell, tuple(tally))
    begin = jnp.int32(0)
    for member in range(members):
        table[4, member] = begin
        ends[member] = begin
        begin = begin + tally[member]
    table[4, members] = begin
    for lag in range(lags):

        def note(slot, carry, lag=lag):
            col = cols[0, 0, lag, slot]
            target = rows[0, 0, lag, slot]
            owner = target // per_owner
            half = lax.bitwise_xor(owner % 2, core) * col_size + owner // 2
            source = lax.bitwise_xor(col // local_blocks, row)
            filled = ends[source]
            ends[source] = filled + 1
            table[0, filled] = lag
            table[1, filled] = half * per_owner + target % per_owner
            table[2, filled] = col % local_blocks
            table[3, filled] = jnp.minimum(places[lag, col], cap - 1)
            held[filled] = tiles[lag, slot]
            return carry

        lax.fori_loop(0, counts[0, 0, lag], note, 0)


def make_plan(cols, rows, counts, needs, tiles, cap, col_size, per_owner):
    lags, total = needs[0].shape
    count = lags * cols.shape[3]
    held = jax.ShapeDtypeStruct((count,) + tiles.shape[2:], tiles.dtype)
    return pl.pallas_call(
        functools.partial(plan_kernel, cap, col_size, per_owner),
        out_shape=[
            jax.ShapeDtypeStruct((5, count), jnp.int32),
            held,
        ],
        in_specs=[SMEM] * (3 + len(needs)) + [VMEM],
        out_specs=[SMEM, VMEM],
        scratch_shapes=[pltpu.SMEM((lags, total), jnp.int32), pltpu.SMEM((len(needs),), jnp.int32)],
        compiler_params=params(tiles, held),
        name="plan_tiles",
    )(cols, rows, counts, *needs, tiles)


def tiles_kernel(first, whole, extra, table, tiles, history, *refs):
    received, (sums, *given), blocks = refs[: len(refs) - 2 - SPLIT - extra], refs[-2 - SPLIT : -1], refs[-1]
    side = tiles.shape[2]
    halves, part, _ = sums.shape
    live = table[4, len(received) + 1]
    sums[...] = jnp.zeros_like(sums)

    def fetch(source):
        def one(index, carry):
            lanes = pl.ds(pl.multiple_of(table[2, index] * side, side), side)
            if source == 0:
                blocks[index] = history[table[0, index], pl.ds(first, part), lanes]
            elif whole:
                blocks[index] = received[source - 1][table[0, index], pl.ds(first, part), lanes]
            else:
                blocks[index] = received[source - 1][table[3, index]]
            return carry

        return one

    for source in range(len(received) + 1):
        lax.fori_loop(table[4, source], table[4, source + 1], fetch(source), 0)

    def multiply(group, carry):
        products = []
        for offset in range(GROUP):
            index = jnp.minimum(group * GROUP + offset, live - 1)
            products.append(
                lax.dot_general(
                    blocks[index], tiles[index], (((1,), (1,)), ((), ())), preferred_element_type=jnp.float32
                )
            )
        for offset, product in enumerate(products):
            index = group * GROUP + offset
            spot = table[1, jnp.minimum(index, live - 1)]
            sums[spot] += product if offset == 0 else jnp.where(index < live, product, 0.0)
        return carry

    lax.fori_loop(0, (live + GROUP - 1) // GROUP, multiply, 0)
    half = halves // 2
    size = half // SPLIT
    flag = jnp.full((1, side), 1.0, jnp.float32) * table[4, OVER].astype(jnp.float32)
    for index, target in enumerate(given):
        exponents = []
        for chunk in range(size):
            grid, exponent = to_fixed(sums[half + index * size + chunk])
            target[chunk * part : (chunk + 1) * part] = grid
            exponents.append(exponent)
        exponents += [jnp.zeros((PAD - 1 - size, side), jnp.float32), flag]
        tail = jnp.concatenate(exponents, axis=0)
        target[size * part :] = tail.astype(jnp.int32).astype(jnp.int16)


def multiply_tiles(first, part, whole, table, tiles, history, received, chunks, after):
    side = tiles.shape[2]
    more = [jax.ShapeDtypeStruct((chunks // SPLIT * part + PAD, side), jnp.int16)] * SPLIT
    blocks = pltpu.VMEM((table.shape[1], part, side), history.dtype)
    sums = jax.ShapeDtypeStruct((2 * chunks, part, side), jnp.float32)
    return pl.pallas_call(
        functools.partial(tiles_kernel, first, whole, len(after)),
        out_shape=[sums, *more],
        in_specs=[SMEM] + [VMEM] * (2 + len(received)) + [ANY] * len(after),
        out_specs=[VMEM] * (1 + SPLIT),
        scratch_shapes=[blocks],
        compiler_params=params(tiles, history, *received, *more, blocks, sums),
        name="multiply_tiles",
    )(table, tiles, history, *received, *after)


def to_fixed(value):
    largest = jnp.maximum(jnp.max(jnp.abs(value), axis=0, keepdims=True), 1e-30)
    exponent = jnp.ceil(jnp.log2(largest))
    grid = jnp.clip(jnp.round(value * jnp.exp2(15.0 - exponent)), -32767.0, 32767.0)
    return grid.astype(jnp.int32).astype(jnp.int16), exponent


def from_fixed(grid, exponent):
    return grid.astype(jnp.int32).astype(jnp.float32) * jnp.exp2(exponent - 15.0)


def code_kernel(per_owner, extra, table, kept, *refs):
    got, own, coded = refs[:SPLIT], refs[SPLIT + extra], refs[SPLIT + extra + 1 : -1]
    theirs = refs[-1]
    chunks, part, side = theirs.shape
    size = chunks // SPLIT
    flag = table[4, OVER].astype(jnp.float32)
    for index, source in enumerate(got):
        tail = source[size * part :, :].astype(jnp.int32).astype(jnp.float32)
        flag = jnp.maximum(flag, tail[PAD - 1 :, :LANES])
        for chunk in range(size):
            theirs[index * size + chunk] = from_fixed(
                source[chunk * part : (chunk + 1) * part, :], tail[chunk : chunk + 1, :]
            )
    col = lax.axis_index("col")
    for step in list(range(1, chunks // per_owner)) + [0]:
        chunk = lax.bitwise_xor(col, step) * per_owner
        exponents = []
        for block in range(per_owner):
            value = kept[chunk + block] + theirs[chunk + block]
            if step == 0:
                own[block] = value
                continue
            out = coded[step - 1]
            grid, exponent = to_fixed(value)
            for lane in range(side // LANES):
                at = len(exponents)
                out[pl.ds(at * part, part), :] = grid[:, lane * LANES : (lane + 1) * LANES]
                exponents.append(exponent[:, lane * LANES : (lane + 1) * LANES])
        if step > 0:
            at = len(exponents)
            exponents.append(jnp.zeros((PAD - 1 - at, LANES), jnp.float32))
            exponents.append(flag)
            tail = jnp.concatenate(exponents, axis=0)
            out[pl.ds(at * part, PAD), :] = tail.astype(jnp.int32).astype(jnp.int16)


def code(table, kept, got, per_owner, after):
    chunks, part, side = kept.shape
    chunks = chunks // 2
    chunk = jax.ShapeDtypeStruct((per_owner * part * (side // LANES) + PAD, LANES), jnp.int16)
    own = jax.ShapeDtypeStruct((per_owner, part, side), jnp.float32)
    outs = [own] + [chunk] * (chunks // per_owner - 1)
    return pl.pallas_call(
        functools.partial(code_kernel, per_owner, len(after)),
        out_shape=outs,
        in_specs=[SMEM] + [VMEM] * (1 + len(got)) + [ANY] * len(after),
        out_specs=[VMEM] * len(outs),
        scratch_shapes=[pltpu.VMEM((chunks, part, side), jnp.float32)],
        compiler_params=params(kept, kept, *got, *outs),
        name="add_and_code",
    )(table, kept, *got, *after)


def solve_kernel(first, fresh, *refs):
    refs, (stress_out, rate_out, stress_held, rate_held, sems) = refs[:-5], refs[-5:]
    if fresh:
        table, *refs, flag_out = refs
    else:
        refs = refs[2:]
    base, rate, direct, state, own, *codes = refs
    per_owner, part, side = own.shape
    rows = pl.ds(first, part)
    tails = [chunk[pl.ds(chunk.shape[0] - PAD, PAD), :].astype(jnp.int32).astype(jnp.float32) for chunk in codes]
    if fresh:
        flag = table[4, OVER].astype(jnp.float32)
        for tail in tails:
            flag = jnp.maximum(flag, jnp.max(tail[PAD - 1 :, :]))
        flag_out[0] = flag.astype(jnp.int32)
    count = per_owner * (side // LANES)
    copies = []
    for at in range(count):
        block, lane = at // (side // LANES), at % (side // LANES)
        stress = own[block, :, pl.ds(lane * LANES, LANES)]
        for chunk, tail in zip(codes, tails):
            stress = stress + from_fixed(chunk[pl.ds(at * part, part), :], tail[at : at + 1, :])
        stress_held[:, pl.ds(at * LANES, LANES)] = stress
    copies.append(pltpu.make_async_copy(stress_held, stress_out.at[rows], sems.at[0]))
    copies[-1].start()
    for at in range(count):
        lanes = pl.ds(at * LANES, LANES)
        rate_held[:, lanes] = friction(
            stress_held[:, lanes], base[rows, lanes], rate[rows, lanes], direct[rows, lanes], state[rows, lanes]
        )
    copies.append(pltpu.make_async_copy(rate_held, rate_out.at[rows], sems.at[1]))
    copies[-1].start()
    for copy in copies:
        copy.wait()


def solve(first, table, fields, own, coded, before):
    sims, owned = fields[0].shape
    part = own.shape[1]
    fresh = before is None
    field = jax.ShapeDtypeStruct(fields[0].shape, jnp.float32)
    held = pltpu.VMEM((part, owned), jnp.float32)
    flag = [jax.ShapeDtypeStruct((1,), jnp.int32)] if fresh else []
    results = pl.pallas_call(
        functools.partial(solve_kernel, first, fresh),
        out_shape=flag + [field, field],
        in_specs=([SMEM] if fresh else [ANY, ANY]) + [VMEM] * (5 + len(coded)),
        out_specs=[SMEM] * len(flag) + [ANY, ANY],
        input_output_aliases={} if fresh else {0: 0, 1: 1},
        scratch_shapes=[held, held, pltpu.SemaphoreType.DMA((2,))],
        compiler_params=params(*fields, own, held, held, *coded),
        name="friction_solve",
    )(*([table] if fresh else before), *fields, own, *coded)
    return results[:-2], results[-2:]


def reduce(first, table, fields, kept, given, before, after):
    per_owner = fields[0].shape[1] // kept.shape[2]
    col_size = lax.axis_size("col")
    got = [lax.ppermute(array, "lag", partners(lax.axis_size("lag"), 1)) for array in given]
    own, *coded = code(table, kept, got, per_owner, after)
    arrived = [
        lax.ppermute(coded[step - 1], "col", partners(col_size, step)) for step in [*range(2, col_size), 1]
    ]
    return solve(first, table, fields, own, arrived, before), (arrived[0], arrived[1]), tuple(arrived)


def local(history, kernel_tiles, tile_rows, tile_cols, tile_count, base_stress, prev_rate, direct_effect, state_var):
    _, _, lags, slots, side, _ = kernel_tiles.shape
    row_size, col_size = (lax.axis_size(axis) for axis in ("row", "col"))
    history = history[:, 0]
    tiles = kernel_tiles[0, 0]
    sims = history.shape[1]
    pieces = []
    for eighths in PIECES:
        pieces.append((sum(part for _, part in pieces), sims * eighths // 8))
    local_blocks = history.shape[2] // side
    total = row_size * local_blocks
    per_owner = base_stress.shape[1] // side
    chunks = col_size * per_owner
    cap = min(CAP, lags * local_blocks)
    fields = (base_stress, prev_rate, direct_effect, state_var)

    need = make_request(tile_cols, tile_count, total)
    requests = [lax.ppermute(need, "row", partners(row_size, step)) for step in range(1, row_size)]
    held = load(history)
    received = []
    for piece in pieces:
        packed = pack(requests, held, side, cap, piece, received[-1][:WAIT] if received else ())
        received.append(
            [lax.ppermute(packed[step - 1], "row", partners(row_size, step)) for step in range(1, row_size)]
        )
    table, live_tiles = make_plan(
        tile_cols, tile_rows, tile_count, [need, *requests], tiles, cap, col_size, per_owner
    )

    after = ()
    flags = result = None
    for (first, part), blocks in zip(pieces, received):
        kept, *given = multiply_tiles(
            first, part, False, table, live_tiles, held, blocks, chunks, after
        )
        (flag, result), after, _ = reduce(first, table, fields, kept, given, result, ())
        flags = flags or flag

    def general():
        everything = [lax.ppermute(history, "row", partners(row_size, step)) for step in range(1, row_size)]
        kept, *given = multiply_tiles(
            0, sims, True, table, live_tiles, history, everything, chunks, ()
        )
        return tuple(reduce(0, table, fields, kept, given, None, ())[0][1])

    return lax.cond(flags[0][0] > 0, general, lambda: tuple(result))


def solution(mesh):
    return jax.shard_map(
        local,
        mesh=mesh,
        in_specs=(
            P("lag", "col", None, "row"),
            P("row", "col", "lag", None, None, None),
            P("row", "col", "lag", None),
            P("row", "col", "lag", None),
            P("row", "col", "lag"),
            P(None, ("row", "col", "lag")),
            P(None, ("row", "col", "lag")),
            P(None, ("row", "col", "lag")),
            P(None, ("row", "col", "lag")),
        ),
        out_specs=(P(None, ("row", "col", "lag")), P(None, ("row", "col", "lag"))),
        check_vma=False,
    )
```

```python
import functools
import math

import jax
import jax.numpy as jnp
from jax import lax
from jax.experimental import pallas as pl
from jax.experimental.pallas import tpu as pltpu
from jax.sharding import PartitionSpec as P

NEWTON = 4
CAP = 16
PIECES = (4, 4)
PAD = 16
LANES = 128
OVER = 16
SPLIT = 2
WAIT = 1
GROUP = 8
ANY = pl.BlockSpec(memory_space=pl.ANY)
SMEM = pl.BlockSpec(memory_space=pltpu.SMEM)
VMEM = pl.BlockSpec(memory_space=pltpu.VMEM)


def params(*shapes):
    held = sum(math.prod(s.shape) * jnp.dtype(s.dtype).itemsize for s in shapes)
    return pltpu.CompilerParams(vmem_limit_bytes=held + 8 * 1024 * 1024)


def padded(rows):
    return (rows // PAD + 1) * PAD


def partners(size, step):
    return [(index, index ^ step) for index in range(size)]


def friction(stress, base, velocity, direct, state):
    driving = base + stress
    factor = jnp.exp(state) / 2.0
    gain = direct * factor
    for step in range(NEWTON):
        scaled = velocity * factor
        square = 1.0 + scaled * scaled
        inverse = lax.rsqrt(square)
        length = jnp.log(jnp.abs(scaled) + square * inverse)
        misfit = direct * jnp.where(scaled < 0.0, -length, length) + 0.5 * velocity - driving
        velocity = velocity - misfit / (gain * inverse + 0.5)
    return velocity


def request_kernel(cols, counts, need):
    lags, total = need.shape
    slots = cols.shape[3]
    names = lax.broadcasted_iota(jnp.int32, (1, total), 1)
    for lag in range(lags):
        marks = jnp.zeros((1, total), jnp.int32)
        for slot in range(slots):
            marks = jnp.where(
                (names == cols[0, 0, lag, slot]) & (slot < counts[0, 0, lag]), 1, marks
            )
        need[lag : lag + 1, :] = marks


def make_request(cols, counts, total):
    return pl.pallas_call(
        request_kernel,
        out_shape=jax.ShapeDtypeStruct((cols.shape[2], total), jnp.int32),
        in_specs=[SMEM, SMEM],
        out_specs=VMEM,
        name="mark_blocks",
    )(cols, counts)


def load_kernel(history, held, sem):
    copy = pltpu.make_async_copy(history, held, sem)
    copy.start()
    copy.wait()


def load(history):
    return pl.pallas_call(
        load_kernel,
        out_shape=history,
        in_specs=[ANY],
        out_specs=VMEM,
        scratch_shapes=[pltpu.SemaphoreType.DMA],
        compiler_params=params(history),
        name="load_history",
    )(history)


def pack_kernel(cap, piece, side, extra, *refs):
    begin, part = piece
    peers = (len(refs) - 1 - extra) // 2
    needs, history, packed = refs[:peers], refs[peers], refs[peers + 1 + extra :]
    lags, sims, width = history.shape
    local_blocks = width // side
    first = lax.axis_index("row") * local_blocks
    for peer in range(peers):
        position = jnp.int32(0)
        for lag in range(lags):
            for block in range(local_blocks):
                wanted = needs[peer][lag, first + block]

                @pl.when((wanted > 0) & (position < cap))
                def _(peer=peer, lag=lag, block=block, position=position):
                    packed[peer][position] = history[
                        lag, begin : begin + part, block * side : (block + 1) * side
                    ]

                position = position + wanted


def pack(needs, history, side, cap, piece, after):
    outs = [jax.ShapeDtypeStruct((cap, piece[1], side), history.dtype)] * len(needs)
    return pl.pallas_call(
        functools.partial(pack_kernel, cap, piece, side, len(after)),
        out_shape=outs,
        in_specs=[SMEM] * len(needs) + [VMEM] + [ANY] * len(after),
        out_specs=[VMEM] * len(outs),
        compiler_params=params(history, *outs),
        name="pack_history",
    )(*needs, history, *after)


def plan_kernel(cap, col_size, per_owner, cols, rows, counts, *refs):
    needs, tiles, (table, held, places, ends) = refs[:-5], refs[-5], refs[-4:]
    lags, total = needs[0].shape
    row, core = lax.axis_index("row"), lax.axis_index("lag")
    members = len(needs)
    local_blocks = total // members
    for owner in range(members):
        position = jnp.int32(0)
        for lag in range(lags):
            for block in range(owner * local_blocks, (owner + 1) * local_blocks):
                places[lag, block] = position
                position = position + needs[0][lag, block]
    above = jnp.int32(0)
    for member in range(members):
        for owner in range(members):
            wanted = jnp.int32(0)
            for lag in range(lags):
                for block in range(local_blocks):
                    wanted = wanted + needs[member][lag, owner * local_blocks + block]
            foreign = lax.bitwise_xor(row, member) != owner
            above = jnp.where(foreign & (wanted > cap), 1, above)
    table[4, OVER] = above
    tally = [jnp.int32(0)] * members
    for lag in range(lags):

        def tell(slot, tally, lag=lag):
            source = lax.bitwise_xor(cols[0, 0, lag, slot] // local_blocks, row)
            return tuple(count + (source == index).astype(jnp.int32) for index, count in enumerate(tally))

        tally = lax.fori_loop(0, counts[0, 0, lag], tell, tuple(tally))
    begin = jnp.int32(0)
    for member in range(members):
        table[4, member] = begin
        ends[member] = begin
        begin = begin + tally[member]
    table[4, members] = begin
    for lag in range(lags):

        def note(slot, carry, lag=lag):
            col = cols[0, 0, lag, slot]
            target = rows[0, 0, lag, slot]
            owner = target // per_owner
            half = lax.bitwise_xor(owner % 2, core) * col_size + owner // 2
            source = lax.bitwise_xor(col // local_blocks, row)
            filled = ends[source]
            ends[source] = filled + 1
            table[0, filled] = lag
            table[1, filled] = half * per_owner + target % per_owner
            table[2, filled] = col % local_blocks
            table[3, filled] = jnp.minimum(places[lag, col], cap - 1)
            held[filled] = tiles[lag, slot]
            return carry

        lax.fori_loop(0, counts[0, 0, lag], note, 0)


def make_plan(cols, rows, counts, needs, tiles, cap, col_size, per_owner):
    lags, total = needs[0].shape
    count = lags * cols.shape[3]
    held = jax.ShapeDtypeStruct((count,) + tiles.shape[2:], tiles.dtype)
    return pl.pallas_call(
        functools.partial(plan_kernel, cap, col_size, per_owner),
        out_shape=[
            jax.ShapeDtypeStruct((5, count), jnp.int32),
            held,
        ],
        in_specs=[SMEM] * (3 + len(needs)) + [VMEM],
        out_specs=[SMEM, VMEM],
        scratch_shapes=[pltpu.SMEM((lags, total), jnp.int32), pltpu.SMEM((len(needs),), jnp.int32)],
        compiler_params=params(tiles, held),
        name="plan_tiles",
    )(cols, rows, counts, *needs, tiles)


def tiles_kernel(first, whole, extra, split, table, tiles, history, *refs):
    received, (sums, *given), blocks = refs[: len(refs) - 2 - split - extra], refs[-2 - split : -1], refs[-1]
    side = tiles.shape[2]
    halves, part, _ = sums.shape
    live = table[4, len(received) + 1]
    sums[...] = jnp.zeros_like(sums)

    def fetch(source):
        def one(index, carry):
            lanes = pl.ds(pl.multiple_of(table[2, index] * side, side), side)
            if source == 0:
                blocks[index] = history[table[0, index], pl.ds(first, part), lanes]
            elif whole:
                blocks[index] = received[source - 1][table[0, index], pl.ds(first, part), lanes]
            else:
                blocks[index] = received[source - 1][table[3, index]]
            return carry

        return one

    for source in range(len(received) + 1):
        lax.fori_loop(table[4, source], table[4, source + 1], fetch(source), 0)

    def multiply(group, carry):
        products = []
        for offset in range(GROUP):
            index = jnp.minimum(group * GROUP + offset, live - 1)
            products.append(
                lax.dot_general(
                    blocks[index], tiles[index], (((1,), (1,)), ((), ())), preferred_element_type=jnp.float32
                )
            )
        for offset, product in enumerate(products):
            index = group * GROUP + offset
            spot = table[1, jnp.minimum(index, live - 1)]
            sums[spot] += product if offset == 0 else jnp.where(index < live, product, 0.0)
        return carry

    lax.fori_loop(0, (live + GROUP - 1) // GROUP, multiply, 0)
    half = halves // 2
    size = half // split
    flag = jnp.full((1, side), 1.0, jnp.float32) * table[4, OVER].astype(jnp.float32)
    for index, target in enumerate(given):
        exponents = []
        for chunk in range(size):
            grid, exponent = to_fixed(sums[half + index * size + chunk])
            target[chunk * part : (chunk + 1) * part] = grid
            exponents.append(exponent)
        exponents += [jnp.zeros((padded(size) - 1 - size, side), jnp.float32), flag]
        tail = jnp.concatenate(exponents, axis=0)
        target[size * part :] = tail.astype(jnp.int32).astype(jnp.int16)


def multiply_tiles(first, part, whole, split, table, tiles, history, received, chunks, after):
    side = tiles.shape[2]
    more = [jax.ShapeDtypeStruct((chunks // split * part + padded(chunks // split), side), jnp.int16)] * split
    blocks = pltpu.VMEM((table.shape[1], part, side), history.dtype)
    sums = jax.ShapeDtypeStruct((2 * chunks, part, side), jnp.float32)
    return pl.pallas_call(
        functools.partial(tiles_kernel, first, whole, len(after), split),
        out_shape=[sums, *more],
        in_specs=[SMEM] + [VMEM] * (2 + len(received)) + [ANY] * len(after),
        out_specs=[VMEM] * (1 + split),
        scratch_shapes=[blocks],
        compiler_params=params(tiles, history, *received, *more, blocks, sums),
        name="multiply_tiles",
    )(table, tiles, history, *received, *after)


def to_fixed(value):
    largest = jnp.maximum(jnp.max(jnp.abs(value), axis=0, keepdims=True), 1e-30)
    exponent = jnp.ceil(jnp.log2(largest))
    grid = jnp.clip(jnp.round(value * jnp.exp2(15.0 - exponent)), -32767.0, 32767.0)
    return grid.astype(jnp.int32).astype(jnp.int16), exponent


def from_fixed(grid, exponent):
    return grid.astype(jnp.int32).astype(jnp.float32) * jnp.exp2(exponent - 15.0)


def code_kernel(per_owner, split, given, kept, *refs):
    got, own, coded, theirs = refs[:split], refs[split], refs[split + 1 : -1], refs[-1]
    chunks, part, side = theirs.shape
    size = chunks // split
    flag = given[given.shape[0] - PAD :, :].astype(jnp.int32).astype(jnp.float32)[PAD - 1 :, :LANES]
    for index, source in enumerate(got):
        tail = source[size * part :, :].astype(jnp.int32).astype(jnp.float32)
        flag = jnp.maximum(flag, tail[padded(size) - 1 :, :LANES])
        for chunk in range(size):
            theirs[index * size + chunk] = from_fixed(
                source[chunk * part : (chunk + 1) * part, :], tail[chunk : chunk + 1, :]
            )
    col = lax.axis_index("col")
    for step in list(range(1, chunks // per_owner)) + [0]:
        chunk = lax.bitwise_xor(col, step) * per_owner
        exponents = []
        for block in range(per_owner):
            value = kept[chunk + block] + theirs[chunk + block]
            if step == 0:
                own[block] = value
                continue
            out = coded[step - 1]
            grid, exponent = to_fixed(value)
            for lane in range(side // LANES):
                at = len(exponents)
                out[pl.ds(at * part, part), :] = grid[:, lane * LANES : (lane + 1) * LANES]
                exponents.append(exponent[:, lane * LANES : (lane + 1) * LANES])
        if step > 0:
            at = len(exponents)
            exponents.append(jnp.zeros((PAD - 1 - at, LANES), jnp.float32))
            exponents.append(flag)
            tail = jnp.concatenate(exponents, axis=0)
            out[pl.ds(at * part, PAD), :] = tail.astype(jnp.int32).astype(jnp.int16)


def code(given, kept, got, per_owner):
    chunks, part, side = kept.shape
    chunks = chunks // 2
    chunk = jax.ShapeDtypeStruct((per_owner * part * (side // LANES) + PAD, LANES), jnp.int16)
    own = jax.ShapeDtypeStruct((per_owner, part, side), jnp.float32)
    outs = [own] + [chunk] * (chunks // per_owner - 1)
    return pl.pallas_call(
        functools.partial(code_kernel, per_owner, len(got)),
        out_shape=outs,
        in_specs=[VMEM] * (2 + len(got)),
        out_specs=[VMEM] * len(outs),
        scratch_shapes=[pltpu.VMEM((chunks, part, side), jnp.float32)],
        compiler_params=params(given, kept, kept, *got, *outs),
        name="add_and_code",
    )(given, kept, *got)


def solve_kernel(first, fresh, *refs):
    refs, (stress_out, rate_out, stress_held, rate_held, sems) = refs[:-5], refs[-5:]
    if fresh:
        table, *refs, flag_out = refs
    else:
        refs = refs[2:]
    base, rate, direct, state, own, *codes = refs
    per_owner, part, side = own.shape
    rows = pl.ds(first, part)
    tails = [chunk[pl.ds(chunk.shape[0] - PAD, PAD), :].astype(jnp.int32).astype(jnp.float32) for chunk in codes]
    if fresh:
        flag = table[4, OVER].astype(jnp.float32)
        for tail in tails:
            flag = jnp.maximum(flag, jnp.max(tail[PAD - 1 :, :]))
        flag_out[0] = flag.astype(jnp.int32)
    count = per_owner * (side // LANES)
    copies = []
    for at in range(count):
        block, lane = at // (side // LANES), at % (side // LANES)
        stress = own[block, :, pl.ds(lane * LANES, LANES)]
        for chunk, tail in zip(codes, tails):
            stress = stress + from_fixed(chunk[pl.ds(at * part, part), :], tail[at : at + 1, :])
        stress_held[:, pl.ds(at * LANES, LANES)] = stress
    copies.append(pltpu.make_async_copy(stress_held, stress_out.at[rows], sems.at[0]))
    copies[-1].start()
    for at in range(count):
        lanes = pl.ds(at * LANES, LANES)
        rate_held[:, lanes] = friction(
            stress_held[:, lanes], base[rows, lanes], rate[rows, lanes], direct[rows, lanes], state[rows, lanes]
        )
    copies.append(pltpu.make_async_copy(rate_held, rate_out.at[rows], sems.at[1]))
    copies[-1].start()
    for copy in copies:
        copy.wait()


def solve(first, table, fields, own, coded, before):
    sims, owned = fields[0].shape
    part = own.shape[1]
    fresh = before is None
    field = jax.ShapeDtypeStruct(fields[0].shape, jnp.float32)
    held = pltpu.VMEM((part, owned), jnp.float32)
    flag = [jax.ShapeDtypeStruct((1,), jnp.int32)] if fresh else []
    results = pl.pallas_call(
        functools.partial(solve_kernel, first, fresh),
        out_shape=flag + [field, field],
        in_specs=([SMEM] if fresh else [ANY, ANY]) + [VMEM] * (5 + len(coded)),
        out_specs=[SMEM] * len(flag) + [ANY, ANY],
        input_output_aliases={} if fresh else {0: 0, 1: 1},
        scratch_shapes=[held, held, pltpu.SemaphoreType.DMA((2,))],
        compiler_params=params(*fields, own, held, held, *coded),
        name="friction_solve",
    )(*([table] if fresh else before), *fields, own, *coded)
    return results[:-2], results[-2:]


def reduce(first, table, fields, kept, given, before):
    per_owner = fields[0].shape[1] // kept.shape[2]
    col_size = lax.axis_size("col")
    got = [lax.ppermute(array, "lag", partners(lax.axis_size("lag"), 1)) for array in given]
    own, *coded = code(given[0], kept, got, per_owner)
    arrived = [
        lax.ppermute(coded[step - 1], "col", partners(col_size, step)) for step in [*range(2, col_size), 1]
    ]
    return solve(first, table, fields, own, arrived, before), (arrived[0], arrived[1]), tuple(arrived)


def local(history, kernel_tiles, tile_rows, tile_cols, tile_count, base_stress, prev_rate, direct_effect, state_var):
    _, _, lags, slots, side, _ = kernel_tiles.shape
    row_size, col_size = (lax.axis_size(axis) for axis in ("row", "col"))
    history = history[:, 0]
    tiles = kernel_tiles[0, 0]
    sims = history.shape[1]
    pieces = []
    for eighths in PIECES:
        pieces.append((sum(part for _, part in pieces), sims * eighths // 8))
    local_blocks = history.shape[2] // side
    total = row_size * local_blocks
    per_owner = base_stress.shape[1] // side
    chunks = col_size * per_owner
    cap = min(CAP, lags * local_blocks)
    fields = (base_stress, prev_rate, direct_effect, state_var)

    need = make_request(tile_cols, tile_count, total)
    requests = [lax.ppermute(need, "row", partners(row_size, step)) for step in range(1, row_size)]
    held = load(history)
    received = []
    for piece in pieces:
        packed = pack(requests, held, side, cap, piece, received[-1][:WAIT] if received else ())
        received.append(
            [lax.ppermute(packed[step - 1], "row", partners(row_size, step)) for step in range(1, row_size)]
        )
    table, live_tiles = make_plan(
        tile_cols, tile_rows, tile_count, [need, *requests], tiles, cap, col_size, per_owner
    )

    after = ()
    flags = result = None
    for (first, part), blocks in zip(pieces, received):
        kept, *given = multiply_tiles(
            first, part, False, 1 if first + part == sims else SPLIT, table, live_tiles, held, blocks, chunks, after
        )
        (flag, result), after, _ = reduce(first, table, fields, kept, given, result)
        flags = flags or flag

    def general():
        everything = [lax.ppermute(history, "row", partners(row_size, step)) for step in range(1, row_size)]
        kept, *given = multiply_tiles(
            0, sims, True, 1, table, live_tiles, history, everything, chunks, ()
        )
        return tuple(reduce(0, table, fields, kept, given, None)[0][1])

    return lax.cond(flags[0][0] > 0, general, lambda: tuple(result))


def solution(mesh):
    return jax.shard_map(
        local,
        mesh=mesh,
        in_specs=(
            P("lag", "col", None, "row"),
            P("row", "col", "lag", None, None, None),
            P("row", "col", "lag", None),
            P("row", "col", "lag", None),
            P("row", "col", "lag"),
            P(None, ("row", "col", "lag")),
            P(None, ("row", "col", "lag")),
            P(None, ("row", "col", "lag")),
            P(None, ("row", "col", "lag")),
        ),
        out_specs=(P(None, ("row", "col", "lag")), P(None, ("row", "col", "lag"))),
        check_vma=False,
    )
```

```python
import functools
import math

import jax
import jax.numpy as jnp
from jax import lax
from jax.experimental import pallas as pl
from jax.experimental.pallas import tpu as pltpu
from jax.sharding import PartitionSpec as P

NEWTON = 4
CAP = 16
PIECES = (4, 4)
PAD = 16
LANES = 128
OVER = 16
SPLIT = 2
GROUP = 8
ANY = pl.BlockSpec(memory_space=pl.ANY)
SMEM = pl.BlockSpec(memory_space=pltpu.SMEM)
VMEM = pl.BlockSpec(memory_space=pltpu.VMEM)


def params(*shapes):
    held = sum(math.prod(s.shape) * jnp.dtype(s.dtype).itemsize for s in shapes)
    return pltpu.CompilerParams(vmem_limit_bytes=held + 8 * 1024 * 1024)


def padded(rows):
    return (rows // PAD + 1) * PAD


def partners(size, step):
    return [(index, index ^ step) for index in range(size)]


def friction(stress, base, velocity, direct, state):
    driving = base + stress
    factor = jnp.exp(state) / 2.0
    gain = direct * factor
    for step in range(NEWTON):
        scaled = velocity * factor
        square = 1.0 + scaled * scaled
        inverse = lax.rsqrt(square)
        length = jnp.log(jnp.abs(scaled) + square * inverse)
        misfit = direct * jnp.where(scaled < 0.0, -length, length) + 0.5 * velocity - driving
        velocity = velocity - misfit / (gain * inverse + 0.5)
    return velocity


def request_kernel(cols, counts, need):
    lags, total = need.shape
    slots = cols.shape[3]
    names = lax.broadcasted_iota(jnp.int32, (1, total), 1)
    for lag in range(lags):
        marks = jnp.zeros((1, total), jnp.int32)
        for slot in range(slots):
            marks = jnp.where(
                (names == cols[0, 0, lag, slot]) & (slot < counts[0, 0, lag]), 1, marks
            )
        need[lag : lag + 1, :] = marks


def make_request(cols, counts, total):
    return pl.pallas_call(
        request_kernel,
        out_shape=jax.ShapeDtypeStruct((cols.shape[2], total), jnp.int32),
        in_specs=[SMEM, SMEM],
        out_specs=VMEM,
        name="mark_blocks",
    )(cols, counts)


def load_kernel(history, held, sem):
    copy = pltpu.make_async_copy(history, held, sem)
    copy.start()
    copy.wait()


def load(history):
    return pl.pallas_call(
        load_kernel,
        out_shape=history,
        in_specs=[ANY],
        out_specs=VMEM,
        scratch_shapes=[pltpu.SemaphoreType.DMA],
        compiler_params=params(history),
        name="load_history",
    )(history)


def pack_kernel(cap, piece, side, extra, *refs):
    begin, part = piece
    peers = (len(refs) - 1 - extra) // 2
    needs, history, packed = refs[:peers], refs[peers], refs[peers + 1 + extra :]
    lags, sims, width = history.shape
    local_blocks = width // side
    first = lax.axis_index("row") * local_blocks
    for peer in range(peers):
        position = jnp.int32(0)
        for lag in range(lags):
            for block in range(local_blocks):
                wanted = needs[peer][lag, first + block]

                @pl.when((wanted > 0) & (position < cap))
                def _(peer=peer, lag=lag, block=block, position=position):
                    packed[peer][position] = history[
                        lag, begin : begin + part, block * side : (block + 1) * side
                    ]

                position = position + wanted


def pack(needs, history, side, cap, piece, after):
    outs = [jax.ShapeDtypeStruct((cap, piece[1], side), history.dtype)] * len(needs)
    return pl.pallas_call(
        functools.partial(pack_kernel, cap, piece, side, len(after)),
        out_shape=outs,
        in_specs=[SMEM] * len(needs) + [VMEM] + [ANY] * len(after),
        out_specs=[VMEM] * len(outs),
        compiler_params=params(history, *outs),
        name="pack_history",
    )(*needs, history, *after)


def plan_kernel(cap, col_size, per_owner, cols, rows, counts, *refs):
    needs, tiles, (table, held, places, ends) = refs[:-5], refs[-5], refs[-4:]
    lags, total = needs[0].shape
    row, core = lax.axis_index("row"), lax.axis_index("lag")
    members = len(needs)
    local_blocks = total // members
    for owner in range(members):
        position = jnp.int32(0)
        for lag in range(lags):
            for block in range(owner * local_blocks, (owner + 1) * local_blocks):
                places[lag, block] = position
                position = position + needs[0][lag, block]
    above = jnp.int32(0)
    for member in range(members):
        for owner in range(members):
            wanted = jnp.int32(0)
            for lag in range(lags):
                for block in range(local_blocks):
                    wanted = wanted + needs[member][lag, owner * local_blocks + block]
            foreign = lax.bitwise_xor(row, member) != owner
            above = jnp.where(foreign & (wanted > cap), 1, above)
    table[4, OVER] = above
    tally = [jnp.int32(0)] * members
    for lag in range(lags):

        def tell(slot, tally, lag=lag):
            source = lax.bitwise_xor(cols[0, 0, lag, slot] // local_blocks, row)
            return tuple(count + (source == index).astype(jnp.int32) for index, count in enumerate(tally))

        tally = lax.fori_loop(0, counts[0, 0, lag], tell, tuple(tally))
    begin = jnp.int32(0)
    for member in range(members):
        table[4, member] = begin
        ends[member] = begin
        begin = begin + tally[member]
    table[4, members] = begin
    for lag in range(lags):

        def note(slot, carry, lag=lag):
            col = cols[0, 0, lag, slot]
            target = rows[0, 0, lag, slot]
            owner = target // per_owner
            half = lax.bitwise_xor(owner % 2, core) * col_size + owner // 2
            source = lax.bitwise_xor(col // local_blocks, row)
            filled = ends[source]
            ends[source] = filled + 1
            table[0, filled] = lag
            table[1, filled] = half * per_owner + target % per_owner
            table[2, filled] = col % local_blocks
            table[3, filled] = jnp.minimum(places[lag, col], cap - 1)
            held[filled] = tiles[lag, slot]
            return carry

        lax.fori_loop(0, counts[0, 0, lag], note, 0)


def make_plan(cols, rows, counts, needs, tiles, cap, col_size, per_owner):
    lags, total = needs[0].shape
    count = lags * cols.shape[3]
    held = jax.ShapeDtypeStruct((count,) + tiles.shape[2:], tiles.dtype)
    return pl.pallas_call(
        functools.partial(plan_kernel, cap, col_size, per_owner),
        out_shape=[
            jax.ShapeDtypeStruct((5, count), jnp.int32),
            held,
        ],
        in_specs=[SMEM] * (3 + len(needs)) + [VMEM],
        out_specs=[SMEM, VMEM],
        scratch_shapes=[pltpu.SMEM((lags, total), jnp.int32), pltpu.SMEM((len(needs),), jnp.int32)],
        compiler_params=params(tiles, held),
        name="plan_tiles",
    )(cols, rows, counts, *needs, tiles)


def add_products(begin, end, table, tiles, blocks, sums):
    def multiply(group, carry):
        products = []
        for offset in range(GROUP):
            index = jnp.minimum(begin + group * GROUP + offset, end - 1)
            products.append(
                lax.dot_general(
                    blocks[index], tiles[index], (((1,), (1,)), ((), ())), preferred_element_type=jnp.float32
                )
            )
        for offset, product in enumerate(products):
            index = begin + group * GROUP + offset
            spot = table[1, jnp.minimum(index, end - 1)]
            sums[spot] += product if offset == 0 else jnp.where(index < end, product, 0.0)
        return carry

    lax.fori_loop(0, (end - begin + GROUP - 1) // GROUP, multiply, 0)


def own_kernel(first, table, tiles, history, sums, blocks):
    side = tiles.shape[2]
    part = sums.shape[1]
    sums[...] = jnp.zeros_like(sums)

    def fetch(index, carry):
        lanes = pl.ds(pl.multiple_of(table[2, index] * side, side), side)
        blocks[index] = history[table[0, index], pl.ds(first, part), lanes]
        return carry

    lax.fori_loop(0, table[4, 1], fetch, 0)
    add_products(0, table[4, 1], table, tiles, blocks, sums)


def tiles_kernel(first, whole, extra, split, table, tiles, begun, *refs):
    received, (sums, *given), blocks = refs[: len(refs) - 2 - split - extra], refs[-2 - split : -1], refs[-1]
    side = tiles.shape[2]
    halves, part, _ = sums.shape
    sums[...] = begun[...]

    def fetch(source):
        def one(index, carry):
            if whole:
                lanes = pl.ds(pl.multiple_of(table[2, index] * side, side), side)
                blocks[index] = received[source - 1][table[0, index], pl.ds(first, part), lanes]
            else:
                blocks[index] = received[source - 1][table[3, index]]
            return carry

        return one

    for source in range(1, len(received) + 1):
        lax.fori_loop(table[4, source], table[4, source + 1], fetch(source), 0)
    add_products(table[4, 1], table[4, len(received) + 1], table, tiles, blocks, sums)
    half = halves // 2
    size = half // split
    flag = jnp.full((1, side), 1.0, jnp.float32) * table[4, OVER].astype(jnp.float32)
    for index, target in enumerate(given):
        exponents = []
        for chunk in range(size):
            grid, exponent = to_fixed(sums[half + index * size + chunk])
            target[chunk * part : (chunk + 1) * part] = grid
            exponents.append(exponent)
        exponents += [jnp.zeros((padded(size) - 1 - size, side), jnp.float32), flag]
        tail = jnp.concatenate(exponents, axis=0)
        target[size * part :] = tail.astype(jnp.int32).astype(jnp.int16)


def multiply_own(first, part, table, tiles, history, chunks):
    side = tiles.shape[2]
    blocks = pltpu.VMEM((table.shape[1], part, side), history.dtype)
    sums = jax.ShapeDtypeStruct((2 * chunks, part, side), jnp.float32)
    return pl.pallas_call(
        functools.partial(own_kernel, first),
        out_shape=sums,
        in_specs=[SMEM, VMEM, VMEM],
        out_specs=VMEM,
        scratch_shapes=[blocks],
        compiler_params=params(tiles, history, blocks, sums),
        name="multiply_own",
    )(table, tiles, history)


def multiply_tiles(first, whole, split, table, tiles, begun, received, after):
    halves, part, side = begun.shape
    chunks = halves // 2
    more = [jax.ShapeDtypeStruct((chunks // split * part + padded(chunks // split), side), jnp.int16)] * split
    blocks = pltpu.VMEM((table.shape[1], part, side), tiles.dtype)
    sums = jax.ShapeDtypeStruct(begun.shape, jnp.float32)
    return pl.pallas_call(
        functools.partial(tiles_kernel, first, whole, len(after), split),
        out_shape=[sums, *more],
        in_specs=[SMEM] + [VMEM] * (2 + len(received)) + [ANY] * len(after),
        out_specs=[VMEM] * (1 + split),
        scratch_shapes=[blocks],
        compiler_params=params(tiles, begun, *received, *more, blocks, sums),
        name="multiply_tiles",
    )(table, tiles, begun, *received, *after)


def to_fixed(value):
    largest = jnp.maximum(jnp.max(jnp.abs(value), axis=0, keepdims=True), 1e-30)
    exponent = jnp.ceil(jnp.log2(largest))
    grid = jnp.clip(jnp.round(value * jnp.exp2(15.0 - exponent)), -32767.0, 32767.0)
    return grid.astype(jnp.int32).astype(jnp.int16), exponent


def from_fixed(grid, exponent):
    return grid.astype(jnp.int32).astype(jnp.float32) * jnp.exp2(exponent - 15.0)


def code_kernel(per_owner, split, given, kept, *refs):
    got, own, coded, theirs = refs[:split], refs[split], refs[split + 1 : -1], refs[-1]
    chunks, part, side = theirs.shape
    size = chunks // split
    flag = given[given.shape[0] - PAD :, :].astype(jnp.int32).astype(jnp.float32)[PAD - 1 :, :LANES]
    for index, source in enumerate(got):
        tail = source[size * part :, :].astype(jnp.int32).astype(jnp.float32)
        flag = jnp.maximum(flag, tail[padded(size) - 1 :, :LANES])
        for chunk in range(size):
            theirs[index * size + chunk] = from_fixed(
                source[chunk * part : (chunk + 1) * part, :], tail[chunk : chunk + 1, :]
            )
    col = lax.axis_index("col")
    for step in list(range(1, chunks // per_owner)) + [0]:
        chunk = lax.bitwise_xor(col, step) * per_owner
        exponents = []
        for block in range(per_owner):
            value = kept[chunk + block] + theirs[chunk + block]
            if step == 0:
                own[block] = value
                continue
            out = coded[step - 1]
            grid, exponent = to_fixed(value)
            for lane in range(side // LANES):
                at = len(exponents)
                out[pl.ds(at * part, part), :] = grid[:, lane * LANES : (lane + 1) * LANES]
                exponents.append(exponent[:, lane * LANES : (lane + 1) * LANES])
        if step > 0:
            at = len(exponents)
            exponents.append(jnp.zeros((PAD - 1 - at, LANES), jnp.float32))
            exponents.append(flag)
            tail = jnp.concatenate(exponents, axis=0)
            out[pl.ds(at * part, PAD), :] = tail.astype(jnp.int32).astype(jnp.int16)


def code(given, kept, got, per_owner):
    chunks, part, side = kept.shape
    chunks = chunks // 2
    chunk = jax.ShapeDtypeStruct((per_owner * part * (side // LANES) + PAD, LANES), jnp.int16)
    own = jax.ShapeDtypeStruct((per_owner, part, side), jnp.float32)
    outs = [own] + [chunk] * (chunks // per_owner - 1)
    return pl.pallas_call(
        functools.partial(code_kernel, per_owner, len(got)),
        out_shape=outs,
        in_specs=[VMEM] * (2 + len(got)),
        out_specs=[VMEM] * len(outs),
        scratch_shapes=[pltpu.VMEM((chunks, part, side), jnp.float32)],
        compiler_params=params(given, kept, kept, *got, *outs),
        name="add_and_code",
    )(given, kept, *got)


def solve_kernel(first, fresh, *refs):
    refs, (stress_out, rate_out, stress_held, rate_held, sems) = refs[:-5], refs[-5:]
    if fresh:
        table, *refs, flag_out = refs
    else:
        refs = refs[2:]
    base, rate, direct, state, own, *codes = refs
    per_owner, part, side = own.shape
    rows = pl.ds(first, part)
    tails = [chunk[pl.ds(chunk.shape[0] - PAD, PAD), :].astype(jnp.int32).astype(jnp.float32) for chunk in codes]
    if fresh:
        flag = table[4, OVER].astype(jnp.float32)
        for tail in tails:
            flag = jnp.maximum(flag, jnp.max(tail[PAD - 1 :, :]))
        flag_out[0] = flag.astype(jnp.int32)
    count = per_owner * (side // LANES)
    copies = []
    for at in range(count):
        block, lane = at // (side // LANES), at % (side // LANES)
        stress = own[block, :, pl.ds(lane * LANES, LANES)]
        for chunk, tail in zip(codes, tails):
            stress = stress + from_fixed(chunk[pl.ds(at * part, part), :], tail[at : at + 1, :])
        stress_held[:, pl.ds(at * LANES, LANES)] = stress
    copies.append(pltpu.make_async_copy(stress_held, stress_out.at[rows], sems.at[0]))
    copies[-1].start()
    for at in range(count):
        lanes = pl.ds(at * LANES, LANES)
        rate_held[:, lanes] = friction(
            stress_held[:, lanes], base[rows, lanes], rate[rows, lanes], direct[rows, lanes], state[rows, lanes]
        )
    copies.append(pltpu.make_async_copy(rate_held, rate_out.at[rows], sems.at[1]))
    copies[-1].start()
    for copy in copies:
        copy.wait()


def solve(first, table, fields, own, coded, before):
    sims, owned = fields[0].shape
    part = own.shape[1]
    fresh = before is None
    field = jax.ShapeDtypeStruct(fields[0].shape, jnp.float32)
    held = pltpu.VMEM((part, owned), jnp.float32)
    flag = [jax.ShapeDtypeStruct((1,), jnp.int32)] if fresh else []
    results = pl.pallas_call(
        functools.partial(solve_kernel, first, fresh),
        out_shape=flag + [field, field],
        in_specs=([SMEM] if fresh else [ANY, ANY]) + [VMEM] * (5 + len(coded)),
        out_specs=[SMEM] * len(flag) + [ANY, ANY],
        input_output_aliases={} if fresh else {0: 0, 1: 1},
        scratch_shapes=[held, held, pltpu.SemaphoreType.DMA((2,))],
        compiler_params=params(*fields, own, held, held, *coded),
        name="friction_solve",
    )(*([table] if fresh else before), *fields, own, *coded)
    return results[:-2], results[-2:]


def reduce(first, table, fields, kept, given, before):
    per_owner = fields[0].shape[1] // kept.shape[2]
    col_size = lax.axis_size("col")
    got = [lax.ppermute(array, "lag", partners(lax.axis_size("lag"), 1)) for array in given]
    own, *coded = code(given[0], kept, got, per_owner)
    arrived = [
        lax.ppermute(coded[step - 1], "col", partners(col_size, step)) for step in [*range(2, col_size), 1]
    ]
    return solve(first, table, fields, own, arrived, before), (arrived[0], arrived[1]), tuple(arrived)


def local(history, kernel_tiles, tile_rows, tile_cols, tile_count, base_stress, prev_rate, direct_effect, state_var):
    _, _, lags, slots, side, _ = kernel_tiles.shape
    row_size, col_size = (lax.axis_size(axis) for axis in ("row", "col"))
    history = history[:, 0]
    tiles = kernel_tiles[0, 0]
    sims = history.shape[1]
    pieces = []
    for eighths in PIECES:
        pieces.append((sum(part for _, part in pieces), sims * eighths // 8))
    local_blocks = history.shape[2] // side
    total = row_size * local_blocks
    per_owner = base_stress.shape[1] // side
    chunks = col_size * per_owner
    cap = min(CAP, lags * local_blocks)
    fields = (base_stress, prev_rate, direct_effect, state_var)

    need = make_request(tile_cols, tile_count, total)
    requests = [lax.ppermute(need, "row", partners(row_size, step)) for step in range(1, row_size)]
    held = load(history)
    table, live_tiles = make_plan(
        tile_cols, tile_rows, tile_count, [need, *requests], tiles, cap, col_size, per_owner
    )

    begun = [multiply_own(first, part, table, live_tiles, held, chunks) for first, part in pieces]
    received = []
    for piece in pieces:
        after = (received[-1][0], *begun) if received else ()
        packed = pack(requests, held, side, cap, piece, after)
        received.append(
            [lax.ppermute(packed[step - 1], "row", partners(row_size, step)) for step in range(1, row_size)]
        )

    after = ()
    flags = result = None
    for (first, part), blocks, own in zip(pieces, received, begun):
        kept, *given = multiply_tiles(
            first, False, 1 if first + part == sims else SPLIT, table, live_tiles, own, blocks, after
        )
        (flag, result), after, _ = reduce(first, table, fields, kept, given, result)
        flags = flags or flag

    def general():
        everything = [lax.ppermute(history, "row", partners(row_size, step)) for step in range(1, row_size)]
        own = multiply_own(0, sims, table, live_tiles, history, chunks)
        kept, *given = multiply_tiles(
            0, True, 1, table, live_tiles, own, everything, ()
        )
        return tuple(reduce(0, table, fields, kept, given, None)[0][1])

    return lax.cond(flags[0][0] > 0, general, lambda: tuple(result))


def solution(mesh):
    return jax.shard_map(
        local,
        mesh=mesh,
        in_specs=(
            P("lag", "col", None, "row"),
            P("row", "col", "lag", None, None, None),
            P("row", "col", "lag", None),
            P("row", "col", "lag", None),
            P("row", "col", "lag"),
            P(None, ("row", "col", "lag")),
            P(None, ("row", "col", "lag")),
            P(None, ("row", "col", "lag")),
            P(None, ("row", "col", "lag")),
        ),
        out_specs=(P(None, ("row", "col", "lag")), P(None, ("row", "col", "lag"))),
        check_vma=False,
    )
```

```python
import functools
import math

import jax
import jax.numpy as jnp
from jax import lax
from jax.experimental import pallas as pl
from jax.experimental.pallas import tpu as pltpu
from jax.sharding import PartitionSpec as P

NEWTON = 4
CAP = 16
PIECES = (4, 4)
PAD = 16
LANES = 128
OVER = 16
SPLIT = 2
GROUP = 8
ANY = pl.BlockSpec(memory_space=pl.ANY)
SMEM = pl.BlockSpec(memory_space=pltpu.SMEM)
VMEM = pl.BlockSpec(memory_space=pltpu.VMEM)


def params(*shapes):
    held = sum(math.prod(s.shape) * jnp.dtype(s.dtype).itemsize for s in shapes)
    return pltpu.CompilerParams(vmem_limit_bytes=held + 8 * 1024 * 1024)


def padded(rows):
    return (rows // PAD + 1) * PAD


def partners(size, step):
    return [(index, index ^ step) for index in range(size)]


def friction(stress, base, velocity, direct, state):
    driving = base + stress
    factor = jnp.exp(state) / 2.0
    gain = direct * factor
    for step in range(NEWTON):
        scaled = velocity * factor
        square = 1.0 + scaled * scaled
        inverse = lax.rsqrt(square)
        length = jnp.log(jnp.abs(scaled) + square * inverse)
        misfit = direct * jnp.where(scaled < 0.0, -length, length) + 0.5 * velocity - driving
        velocity = velocity - misfit / (gain * inverse + 0.5)
    return velocity


def request_kernel(cols, counts, need):
    lags, total = need.shape
    slots = cols.shape[3]
    names = lax.broadcasted_iota(jnp.int32, (1, total), 1)
    for lag in range(lags):
        marks = jnp.zeros((1, total), jnp.int32)
        for slot in range(slots):
            marks = jnp.where(
                (names == cols[0, 0, lag, slot]) & (slot < counts[0, 0, lag]), 1, marks
            )
        need[lag : lag + 1, :] = marks


def make_request(cols, counts, total):
    return pl.pallas_call(
        request_kernel,
        out_shape=jax.ShapeDtypeStruct((cols.shape[2], total), jnp.int32),
        in_specs=[SMEM, SMEM],
        out_specs=VMEM,
        name="mark_blocks",
    )(cols, counts)


def load_kernel(history, held, sem):
    copy = pltpu.make_async_copy(history, held, sem)
    copy.start()
    copy.wait()


def load(history):
    return pl.pallas_call(
        load_kernel,
        out_shape=history,
        in_specs=[ANY],
        out_specs=VMEM,
        scratch_shapes=[pltpu.SemaphoreType.DMA],
        compiler_params=params(history),
        name="load_history",
    )(history)


def pack_kernel(cap, piece, side, extra, *refs):
    begin, part = piece
    peers = (len(refs) - 1 - extra) // 2
    needs, history, packed = refs[:peers], refs[peers], refs[peers + 1 + extra :]
    lags, sims, width = history.shape
    local_blocks = width // side
    first = lax.axis_index("row") * local_blocks
    for peer in range(peers):
        position = jnp.int32(0)
        for lag in range(lags):
            for block in range(local_blocks):
                wanted = needs[peer][lag, first + block]

                @pl.when((wanted > 0) & (position < cap))
                def _(peer=peer, lag=lag, block=block, position=position):
                    packed[peer][position] = history[
                        lag, begin : begin + part, block * side : (block + 1) * side
                    ]

                position = position + wanted


def pack(needs, history, side, cap, piece, after):
    outs = [jax.ShapeDtypeStruct((cap, piece[1], side), history.dtype)] * len(needs)
    return pl.pallas_call(
        functools.partial(pack_kernel, cap, piece, side, len(after)),
        out_shape=outs,
        in_specs=[SMEM] * len(needs) + [VMEM] + [ANY] * len(after),
        out_specs=[VMEM] * len(outs),
        compiler_params=params(history, *outs),
        name="pack_history",
    )(*needs, history, *after)


def plan_kernel(cap, col_size, per_owner, cols, rows, counts, *refs):
    needs, tiles, (table, held, places, ends) = refs[:-5], refs[-5], refs[-4:]
    lags, total = needs[0].shape
    row, core = lax.axis_index("row"), lax.axis_index("lag")
    members = len(needs)
    local_blocks = total // members
    for owner in range(members):
        position = jnp.int32(0)
        for lag in range(lags):
            for block in range(owner * local_blocks, (owner + 1) * local_blocks):
                places[lag, block] = position
                position = position + needs[0][lag, block]
    above = jnp.int32(0)
    for member in range(members):
        for owner in range(members):
            wanted = jnp.int32(0)
            for lag in range(lags):
                for block in range(local_blocks):
                    wanted = wanted + needs[member][lag, owner * local_blocks + block]
            foreign = lax.bitwise_xor(row, member) != owner
            above = jnp.where(foreign & (wanted > cap), 1, above)
    table[4, OVER] = above
    tally = [jnp.int32(0)] * members
    for lag in range(lags):

        def tell(slot, tally, lag=lag):
            source = lax.bitwise_xor(cols[0, 0, lag, slot] // local_blocks, row)
            return tuple(count + (source == index).astype(jnp.int32) for index, count in enumerate(tally))

        tally = lax.fori_loop(0, counts[0, 0, lag], tell, tuple(tally))
    begin = jnp.int32(0)
    for member in range(members):
        table[4, member] = begin
        ends[member] = begin
        begin = begin + tally[member]
    table[4, members] = begin
    for lag in range(lags):

        def note(slot, carry, lag=lag):
            col = cols[0, 0, lag, slot]
            target = rows[0, 0, lag, slot]
            owner = target // per_owner
            half = lax.bitwise_xor(owner % 2, core) * col_size + owner // 2
            source = lax.bitwise_xor(col // local_blocks, row)
            filled = ends[source]
            ends[source] = filled + 1
            table[0, filled] = lag
            table[1, filled] = half * per_owner + target % per_owner
            table[2, filled] = col % local_blocks
            table[3, filled] = jnp.minimum(places[lag, col], cap - 1)
            held[filled] = tiles[lag, slot]
            return carry

        lax.fori_loop(0, counts[0, 0, lag], note, 0)


def make_plan(cols, rows, counts, needs, tiles, cap, col_size, per_owner):
    lags, total = needs[0].shape
    count = lags * cols.shape[3]
    held = jax.ShapeDtypeStruct((count,) + tiles.shape[2:], tiles.dtype)
    return pl.pallas_call(
        functools.partial(plan_kernel, cap, col_size, per_owner),
        out_shape=[
            jax.ShapeDtypeStruct((5, count), jnp.int32),
            held,
        ],
        in_specs=[SMEM] * (3 + len(needs)) + [VMEM],
        out_specs=[SMEM, VMEM],
        scratch_shapes=[pltpu.SMEM((lags, total), jnp.int32), pltpu.SMEM((len(needs),), jnp.int32)],
        compiler_params=params(tiles, held),
        name="plan_tiles",
    )(cols, rows, counts, *needs, tiles)


def add_products(begin, end, table, tiles, blocks, sums):
    def multiply(group, carry):
        products = []
        for offset in range(GROUP):
            index = jnp.minimum(begin + group * GROUP + offset, end - 1)
            products.append(
                lax.dot_general(
                    blocks[index], tiles[index], (((1,), (1,)), ((), ())), preferred_element_type=jnp.float32
                )
            )
        for offset, product in enumerate(products):
            index = begin + group * GROUP + offset
            spot = table[1, jnp.minimum(index, end - 1)]
            sums[spot] += product if offset == 0 else jnp.where(index < end, product, 0.0)
        return carry

    lax.fori_loop(0, (end - begin + GROUP - 1) // GROUP, multiply, 0)


def own_kernel(first, table, tiles, history, sums, blocks):
    side = tiles.shape[2]
    part = sums.shape[1]
    sums[...] = jnp.zeros_like(sums)

    def fetch(index, carry):
        lanes = pl.ds(pl.multiple_of(table[2, index] * side, side), side)
        blocks[index] = history[table[0, index], pl.ds(first, part), lanes]
        return carry

    lax.fori_loop(0, table[4, 1], fetch, 0)
    add_products(0, table[4, 1], table, tiles, blocks, sums)


def early_kernel(table, tiles, begun, received, sums, blocks):
    sums[...] = begun[...]

    def fetch(index, carry):
        blocks[index] = received[table[3, index]]
        return carry

    lax.fori_loop(table[4, 1], table[4, 2], fetch, 0)
    add_products(table[4, 1], table[4, 2], table, tiles, blocks, sums)


def multiply_early(table, tiles, begun, received):
    _, part, side = begun.shape
    blocks = pltpu.VMEM((table.shape[1], part, side), tiles.dtype)
    sums = jax.ShapeDtypeStruct(begun.shape, jnp.float32)
    return pl.pallas_call(
        early_kernel,
        out_shape=sums,
        in_specs=[SMEM, VMEM, VMEM, VMEM],
        out_specs=VMEM,
        scratch_shapes=[blocks],
        compiler_params=params(tiles, begun, received, blocks, sums),
        name="multiply_early",
    )(table, tiles, begun, received)


def tiles_kernel(first, whole, extra, split, table, tiles, begun, *refs):
    received, (sums, *given), blocks = refs[: len(refs) - 2 - split - extra], refs[-2 - split : -1], refs[-1]
    side = tiles.shape[2]
    halves, part, _ = sums.shape
    sums[...] = begun[...]

    def fetch(source):
        def one(index, carry):
            if whole:
                lanes = pl.ds(pl.multiple_of(table[2, index] * side, side), side)
                blocks[index] = received[source - 1][table[0, index], pl.ds(first, part), lanes]
            else:
                blocks[index] = received[source - 1][table[3, index]]
            return carry

        return one

    done = 1 if whole else 2
    last = done + len(received)
    for source in range(done, last):
        lax.fori_loop(table[4, source], table[4, source + 1], fetch(source - done + 1), 0)
    add_products(table[4, done], table[4, last], table, tiles, blocks, sums)
    half = halves // 2
    size = half // split
    flag = jnp.full((1, side), 1.0, jnp.float32) * table[4, OVER].astype(jnp.float32)
    for index, target in enumerate(given):
        exponents = []
        for chunk in range(size):
            grid, exponent = to_fixed(sums[half + index * size + chunk])
            target[chunk * part : (chunk + 1) * part] = grid
            exponents.append(exponent)
        exponents += [jnp.zeros((padded(size) - 1 - size, side), jnp.float32), flag]
        tail = jnp.concatenate(exponents, axis=0)
        target[size * part :] = tail.astype(jnp.int32).astype(jnp.int16)


def multiply_own(first, part, table, tiles, history, chunks):
    side = tiles.shape[2]
    blocks = pltpu.VMEM((table.shape[1], part, side), history.dtype)
    sums = jax.ShapeDtypeStruct((2 * chunks, part, side), jnp.float32)
    return pl.pallas_call(
        functools.partial(own_kernel, first),
        out_shape=sums,
        in_specs=[SMEM, VMEM, VMEM],
        out_specs=VMEM,
        scratch_shapes=[blocks],
        compiler_params=params(tiles, history, blocks, sums),
        name="multiply_own",
    )(table, tiles, history)


def multiply_tiles(first, whole, split, table, tiles, begun, received, after):
    halves, part, side = begun.shape
    chunks = halves // 2
    more = [jax.ShapeDtypeStruct((chunks // split * part + padded(chunks // split), side), jnp.int16)] * split
    blocks = pltpu.VMEM((table.shape[1], part, side), tiles.dtype)
    sums = jax.ShapeDtypeStruct(begun.shape, jnp.float32)
    return pl.pallas_call(
        functools.partial(tiles_kernel, first, whole, len(after), split),
        out_shape=[sums, *more],
        in_specs=[SMEM] + [VMEM] * (2 + len(received)) + [ANY] * len(after),
        out_specs=[VMEM] * (1 + split),
        scratch_shapes=[blocks],
        compiler_params=params(tiles, begun, *received, *more, blocks, sums),
        name="multiply_tiles",
    )(table, tiles, begun, *received, *after)


def to_fixed(value):
    largest = jnp.maximum(jnp.max(jnp.abs(value), axis=0, keepdims=True), 1e-30)
    exponent = jnp.ceil(jnp.log2(largest))
    grid = jnp.clip(jnp.round(value * jnp.exp2(15.0 - exponent)), -32767.0, 32767.0)
    return grid.astype(jnp.int32).astype(jnp.int16), exponent


def from_fixed(grid, exponent):
    return grid.astype(jnp.int32).astype(jnp.float32) * jnp.exp2(exponent - 15.0)


def code_kernel(per_owner, split, given, kept, *refs):
    got, own, coded, theirs = refs[:split], refs[split], refs[split + 1 : -1], refs[-1]
    chunks, part, side = theirs.shape
    size = chunks // split
    flag = given[given.shape[0] - PAD :, :].astype(jnp.int32).astype(jnp.float32)[PAD - 1 :, :LANES]
    for index, source in enumerate(got):
        tail = source[size * part :, :].astype(jnp.int32).astype(jnp.float32)
        flag = jnp.maximum(flag, tail[padded(size) - 1 :, :LANES])
        for chunk in range(size):
            theirs[index * size + chunk] = from_fixed(
                source[chunk * part : (chunk + 1) * part, :], tail[chunk : chunk + 1, :]
            )
    col = lax.axis_index("col")
    for step in list(range(1, chunks // per_owner)) + [0]:
        chunk = lax.bitwise_xor(col, step) * per_owner
        exponents = []
        for block in range(per_owner):
            value = kept[chunk + block] + theirs[chunk + block]
            if step == 0:
                own[block] = value
                continue
            out = coded[step - 1]
            grid, exponent = to_fixed(value)
            for lane in range(side // LANES):
                at = len(exponents)
                out[pl.ds(at * part, part), :] = grid[:, lane * LANES : (lane + 1) * LANES]
                exponents.append(exponent[:, lane * LANES : (lane + 1) * LANES])
        if step > 0:
            at = len(exponents)
            exponents.append(jnp.zeros((PAD - 1 - at, LANES), jnp.float32))
            exponents.append(flag)
            tail = jnp.concatenate(exponents, axis=0)
            out[pl.ds(at * part, PAD), :] = tail.astype(jnp.int32).astype(jnp.int16)


def code(given, kept, got, per_owner):
    chunks, part, side = kept.shape
    chunks = chunks // 2
    chunk = jax.ShapeDtypeStruct((per_owner * part * (side // LANES) + PAD, LANES), jnp.int16)
    own = jax.ShapeDtypeStruct((per_owner, part, side), jnp.float32)
    outs = [own] + [chunk] * (chunks // per_owner - 1)
    return pl.pallas_call(
        functools.partial(code_kernel, per_owner, len(got)),
        out_shape=outs,
        in_specs=[VMEM] * (2 + len(got)),
        out_specs=[VMEM] * len(outs),
        scratch_shapes=[pltpu.VMEM((chunks, part, side), jnp.float32)],
        compiler_params=params(given, kept, kept, *got, *outs),
        name="add_and_code",
    )(given, kept, *got)


def solve_kernel(first, fresh, *refs):
    refs, (stress_out, rate_out, stress_held, rate_held, sems) = refs[:-5], refs[-5:]
    if fresh:
        table, *refs, flag_out = refs
    else:
        refs = refs[2:]
    base, rate, direct, state, own, *codes = refs
    per_owner, part, side = own.shape
    rows = pl.ds(first, part)
    tails = [chunk[pl.ds(chunk.shape[0] - PAD, PAD), :].astype(jnp.int32).astype(jnp.float32) for chunk in codes]
    if fresh:
        flag = table[4, OVER].astype(jnp.float32)
        for tail in tails:
            flag = jnp.maximum(flag, jnp.max(tail[PAD - 1 :, :]))
        flag_out[0] = flag.astype(jnp.int32)
    count = per_owner * (side // LANES)
    copies = []
    for at in range(count):
        block, lane = at // (side // LANES), at % (side // LANES)
        stress = own[block, :, pl.ds(lane * LANES, LANES)]
        for chunk, tail in zip(codes, tails):
            stress = stress + from_fixed(chunk[pl.ds(at * part, part), :], tail[at : at + 1, :])
        stress_held[:, pl.ds(at * LANES, LANES)] = stress
    copies.append(pltpu.make_async_copy(stress_held, stress_out.at[rows], sems.at[0]))
    copies[-1].start()
    for at in range(count):
        lanes = pl.ds(at * LANES, LANES)
        rate_held[:, lanes] = friction(
            stress_held[:, lanes], base[rows, lanes], rate[rows, lanes], direct[rows, lanes], state[rows, lanes]
        )
    copies.append(pltpu.make_async_copy(rate_held, rate_out.at[rows], sems.at[1]))
    copies[-1].start()
    for copy in copies:
        copy.wait()


def solve(first, table, fields, own, coded, before):
    sims, owned = fields[0].shape
    part = own.shape[1]
    fresh = before is None
    field = jax.ShapeDtypeStruct(fields[0].shape, jnp.float32)
    held = pltpu.VMEM((part, owned), jnp.float32)
    flag = [jax.ShapeDtypeStruct((1,), jnp.int32)] if fresh else []
    results = pl.pallas_call(
        functools.partial(solve_kernel, first, fresh),
        out_shape=flag + [field, field],
        in_specs=([SMEM] if fresh else [ANY, ANY]) + [VMEM] * (5 + len(coded)),
        out_specs=[SMEM] * len(flag) + [ANY, ANY],
        input_output_aliases={} if fresh else {0: 0, 1: 1},
        scratch_shapes=[held, held, pltpu.SemaphoreType.DMA((2,))],
        compiler_params=params(*fields, own, held, held, *coded),
        name="friction_solve",
    )(*([table] if fresh else before), *fields, own, *coded)
    return results[:-2], results[-2:]


def reduce(first, table, fields, kept, given, before):
    per_owner = fields[0].shape[1] // kept.shape[2]
    col_size = lax.axis_size("col")
    got = [lax.ppermute(array, "lag", partners(lax.axis_size("lag"), 1)) for array in given]
    own, *coded = code(given[0], kept, got, per_owner)
    arrived = [
        lax.ppermute(coded[step - 1], "col", partners(col_size, step)) for step in [*range(2, col_size), 1]
    ]
    return solve(first, table, fields, own, arrived, before), (arrived[0], arrived[1]), tuple(arrived)


def local(history, kernel_tiles, tile_rows, tile_cols, tile_count, base_stress, prev_rate, direct_effect, state_var):
    _, _, lags, slots, side, _ = kernel_tiles.shape
    row_size, col_size = (lax.axis_size(axis) for axis in ("row", "col"))
    history = history[:, 0]
    tiles = kernel_tiles[0, 0]
    sims = history.shape[1]
    pieces = []
    for eighths in PIECES:
        pieces.append((sum(part for _, part in pieces), sims * eighths // 8))
    local_blocks = history.shape[2] // side
    total = row_size * local_blocks
    per_owner = base_stress.shape[1] // side
    chunks = col_size * per_owner
    cap = min(CAP, lags * local_blocks)
    fields = (base_stress, prev_rate, direct_effect, state_var)

    need = make_request(tile_cols, tile_count, total)
    requests = [lax.ppermute(need, "row", partners(row_size, step)) for step in range(1, row_size)]
    held = load(history)
    table, live_tiles = make_plan(
        tile_cols, tile_rows, tile_count, [need, *requests], tiles, cap, col_size, per_owner
    )

    begun = [multiply_own(first, part, table, live_tiles, held, chunks) for first, part in pieces]
    received = []
    for piece in pieces:
        after = (received[-1][0], *begun) if received else ()
        packed = pack(requests, held, side, cap, piece, after)
        received.append(
            [lax.ppermute(packed[step - 1], "row", partners(row_size, step)) for step in range(1, row_size)]
        )

    after = ()
    flags = result = None
    for (first, part), blocks, own in zip(pieces, received, begun):
        kept, *given = multiply_tiles(
            first, False, 1 if first + part == sims else SPLIT, table, live_tiles, multiply_early(table, live_tiles, own, blocks[0]), blocks[1:], after
        )
        (flag, result), after, _ = reduce(first, table, fields, kept, given, result)
        flags = flags or flag

    def general():
        everything = [lax.ppermute(history, "row", partners(row_size, step)) for step in range(1, row_size)]
        own = multiply_own(0, sims, table, live_tiles, history, chunks)
        kept, *given = multiply_tiles(
            0, True, 1, table, live_tiles, own, everything, ()
        )
        return tuple(reduce(0, table, fields, kept, given, None)[0][1])

    return lax.cond(flags[0][0] > 0, general, lambda: tuple(result))


def solution(mesh):
    return jax.shard_map(
        local,
        mesh=mesh,
        in_specs=(
            P("lag", "col", None, "row"),
            P("row", "col", "lag", None, None, None),
            P("row", "col", "lag", None),
            P("row", "col", "lag", None),
            P("row", "col", "lag"),
            P(None, ("row", "col", "lag")),
            P(None, ("row", "col", "lag")),
            P(None, ("row", "col", "lag")),
            P(None, ("row", "col", "lag")),
        ),
        out_specs=(P(None, ("row", "col", "lag")), P(None, ("row", "col", "lag"))),
        check_vma=False,
    )
```

```python
import functools
import math

import jax
import jax.numpy as jnp
from jax import lax
from jax.experimental import pallas as pl
from jax.experimental.pallas import tpu as pltpu
from jax.sharding import PartitionSpec as P

NEWTON = 4
CAP = 16
PIECES = (4, 4)
PAD = 16
LANES = 128
OVER = 16
SPLIT = 2
GROUP = 6
ANY = pl.BlockSpec(memory_space=pl.ANY)
SMEM = pl.BlockSpec(memory_space=pltpu.SMEM)
VMEM = pl.BlockSpec(memory_space=pltpu.VMEM)


def params(*shapes):
    held = sum(math.prod(s.shape) * jnp.dtype(s.dtype).itemsize for s in shapes)
    return pltpu.CompilerParams(vmem_limit_bytes=held + 8 * 1024 * 1024)


def padded(rows):
    return (rows // PAD + 1) * PAD


def partners(size, step):
    return [(index, index ^ step) for index in range(size)]


def friction(stress, base, velocity, direct, state):
    driving = base + stress
    factor = jnp.exp(state) / 2.0
    gain = direct * factor
    for step in range(NEWTON):
        scaled = velocity * factor
        square = 1.0 + scaled * scaled
        inverse = lax.rsqrt(square)
        length = jnp.log(jnp.abs(scaled) + square * inverse)
        misfit = direct * jnp.where(scaled < 0.0, -length, length) + 0.5 * velocity - driving
        velocity = velocity - misfit / (gain * inverse + 0.5)
    return velocity


def request_kernel(cols, counts, need):
    lags, total = need.shape
    slots = cols.shape[3]
    names = lax.broadcasted_iota(jnp.int32, (1, total), 1)
    for lag in range(lags):
        marks = jnp.zeros((1, total), jnp.int32)
        for slot in range(slots):
            marks = jnp.where(
                (names == cols[0, 0, lag, slot]) & (slot < counts[0, 0, lag]), 1, marks
            )
        need[lag : lag + 1, :] = marks


def make_request(cols, counts, total):
    return pl.pallas_call(
        request_kernel,
        out_shape=jax.ShapeDtypeStruct((cols.shape[2], total), jnp.int32),
        in_specs=[SMEM, SMEM],
        out_specs=VMEM,
        name="mark_blocks",
    )(cols, counts)


def load_kernel(history, held, sem):
    copy = pltpu.make_async_copy(history, held, sem)
    copy.start()
    copy.wait()


def load(history):
    return pl.pallas_call(
        load_kernel,
        out_shape=history,
        in_specs=[ANY],
        out_specs=VMEM,
        scratch_shapes=[pltpu.SemaphoreType.DMA],
        compiler_params=params(history),
        name="load_history",
    )(history)


def pack_kernel(cap, piece, side, extra, *refs):
    begin, part = piece
    peers = (len(refs) - 1 - extra) // 2
    needs, history, packed = refs[:peers], refs[peers], refs[peers + 1 + extra :]
    lags, sims, width = history.shape
    local_blocks = width // side
    first = lax.axis_index("row") * local_blocks
    for peer in range(peers):
        position = jnp.int32(0)
        for lag in range(lags):
            for block in range(local_blocks):
                wanted = needs[peer][lag, first + block]

                @pl.when((wanted > 0) & (position < cap))
                def _(peer=peer, lag=lag, block=block, position=position):
                    packed[peer][position] = history[
                        lag, begin : begin + part, block * side : (block + 1) * side
                    ]

                position = position + wanted


def pack(needs, history, side, cap, piece, after):
    outs = [jax.ShapeDtypeStruct((cap, piece[1], side), history.dtype)] * len(needs)
    return pl.pallas_call(
        functools.partial(pack_kernel, cap, piece, side, len(after)),
        out_shape=outs,
        in_specs=[SMEM] * len(needs) + [VMEM] + [ANY] * len(after),
        out_specs=[VMEM] * len(outs),
        compiler_params=params(history, *outs),
        name="pack_history",
    )(*needs, history, *after)


def plan_kernel(cap, col_size, per_owner, cols, rows, counts, *refs):
    needs, tiles, (table, held, places, ends) = refs[:-5], refs[-5], refs[-4:]
    lags, total = needs[0].shape
    row, core = lax.axis_index("row"), lax.axis_index("lag")
    members = len(needs)
    local_blocks = total // members
    for owner in range(members):
        position = jnp.int32(0)
        for lag in range(lags):
            for block in range(owner * local_blocks, (owner + 1) * local_blocks):
                places[lag, block] = position
                position = position + needs[0][lag, block]
    above = jnp.int32(0)
    for member in range(members):
        for owner in range(members):
            wanted = jnp.int32(0)
            for lag in range(lags):
                for block in range(local_blocks):
                    wanted = wanted + needs[member][lag, owner * local_blocks + block]
            foreign = lax.bitwise_xor(row, member) != owner
            above = jnp.where(foreign & (wanted > cap), 1, above)
    table[4, OVER] = above
    tally = [jnp.int32(0)] * members
    for lag in range(lags):

        def tell(slot, tally, lag=lag):
            source = lax.bitwise_xor(cols[0, 0, lag, slot] // local_blocks, row)
            return tuple(count + (source == index).astype(jnp.int32) for index, count in enumerate(tally))

        tally = lax.fori_loop(0, counts[0, 0, lag], tell, tuple(tally))
    begin = jnp.int32(0)
    for member in range(members):
        table[4, member] = begin
        ends[member] = begin
        begin = begin + tally[member]
    table[4, members] = begin
    for lag in range(lags):

        def note(slot, carry, lag=lag):
            col = cols[0, 0, lag, slot]
            target = rows[0, 0, lag, slot]
            owner = target // per_owner
            half = lax.bitwise_xor(owner % 2, core) * col_size + owner // 2
            source = lax.bitwise_xor(col // local_blocks, row)
            filled = ends[source]
            ends[source] = filled + 1
            table[0, filled] = lag
            table[1, filled] = half * per_owner + target % per_owner
            table[2, filled] = col % local_blocks
            table[3, filled] = jnp.minimum(places[lag, col], cap - 1)
            held[filled] = tiles[lag, slot]
            return carry

        lax.fori_loop(0, counts[0, 0, lag], note, 0)


def make_plan(cols, rows, counts, needs, tiles, cap, col_size, per_owner):
    lags, total = needs[0].shape
    count = lags * cols.shape[3]
    held = jax.ShapeDtypeStruct((count,) + tiles.shape[2:], tiles.dtype)
    return pl.pallas_call(
        functools.partial(plan_kernel, cap, col_size, per_owner),
        out_shape=[
            jax.ShapeDtypeStruct((5, count), jnp.int32),
            held,
        ],
        in_specs=[SMEM] * (3 + len(needs)) + [VMEM],
        out_specs=[SMEM, VMEM],
        scratch_shapes=[pltpu.SMEM((lags, total), jnp.int32), pltpu.SMEM((len(needs),), jnp.int32)],
        compiler_params=params(tiles, held),
        name="plan_tiles",
    )(cols, rows, counts, *needs, tiles)


def add_products(begin, end, table, tiles, blocks, sums):
    def multiply(group, carry):
        products = []
        for offset in range(GROUP):
            index = jnp.minimum(begin + group * GROUP + offset, end - 1)
            products.append(
                lax.dot_general(
                    blocks[index], tiles[index], (((1,), (1,)), ((), ())), preferred_element_type=jnp.float32
                )
            )
        for offset, product in enumerate(products):
            index = begin + group * GROUP + offset
            spot = table[1, jnp.minimum(index, end - 1)]
            sums[spot] += product if offset == 0 else jnp.where(index < end, product, 0.0)
        return carry

    lax.fori_loop(0, (end - begin + GROUP - 1) // GROUP, multiply, 0)


def own_kernel(first, table, tiles, history, sums, blocks):
    side = tiles.shape[2]
    part = sums.shape[1]
    sums[...] = jnp.zeros_like(sums)

    def fetch(index, carry):
        lanes = pl.ds(pl.multiple_of(table[2, index] * side, side), side)
        blocks[index] = history[table[0, index], pl.ds(first, part), lanes]
        return carry

    lax.fori_loop(0, table[4, 1], fetch, 0)
    add_products(0, table[4, 1], table, tiles, blocks, sums)


def early_kernel(table, tiles, begun, received, sums, blocks):
    sums[...] = begun[...]

    def fetch(index, carry):
        blocks[index] = received[table[3, index]]
        return carry

    lax.fori_loop(table[4, 1], table[4, 2], fetch, 0)
    add_products(table[4, 1], table[4, 2], table, tiles, blocks, sums)


def multiply_early(table, tiles, begun, received):
    _, part, side = begun.shape
    blocks = pltpu.VMEM((table.shape[1], part, side), tiles.dtype)
    sums = jax.ShapeDtypeStruct(begun.shape, jnp.float32)
    return pl.pallas_call(
        early_kernel,
        out_shape=sums,
        in_specs=[SMEM, VMEM, VMEM, VMEM],
        out_specs=VMEM,
        scratch_shapes=[blocks],
        compiler_params=params(tiles, begun, received, blocks, sums),
        name="multiply_early",
    )(table, tiles, begun, received)


def tiles_kernel(first, whole, extra, split, table, tiles, begun, *refs):
    received, (sums, *given), blocks = refs[: len(refs) - 2 - split - extra], refs[-2 - split : -1], refs[-1]
    side = tiles.shape[2]
    halves, part, _ = sums.shape
    sums[...] = begun[...]

    def fetch(source):
        def one(index, carry):
            if whole:
                lanes = pl.ds(pl.multiple_of(table[2, index] * side, side), side)
                blocks[index] = received[source - 1][table[0, index], pl.ds(first, part), lanes]
            else:
                blocks[index] = received[source - 1][table[3, index]]
            return carry

        return one

    done = 1 if whole else 2
    last = done + len(received)
    for source in range(done, last):
        lax.fori_loop(table[4, source], table[4, source + 1], fetch(source - done + 1), 0)
    add_products(table[4, done], table[4, last], table, tiles, blocks, sums)
    half = halves // 2
    size = half // split
    flag = jnp.full((1, side), 1.0, jnp.float32) * table[4, OVER].astype(jnp.float32)
    for index, target in enumerate(given):
        exponents = []
        for chunk in range(size):
            grid, exponent = to_fixed(sums[half + index * size + chunk])
            target[chunk * part : (chunk + 1) * part] = grid
            exponents.append(exponent)
        exponents += [jnp.zeros((padded(size) - 1 - size, side), jnp.float32), flag]
        tail = jnp.concatenate(exponents, axis=0)
        target[size * part :] = tail.astype(jnp.int32).astype(jnp.int16)


def multiply_own(first, part, table, tiles, history, chunks):
    side = tiles.shape[2]
    blocks = pltpu.VMEM((table.shape[1], part, side), history.dtype)
    sums = jax.ShapeDtypeStruct((2 * chunks, part, side), jnp.float32)
    return pl.pallas_call(
        functools.partial(own_kernel, first),
        out_shape=sums,
        in_specs=[SMEM, VMEM, VMEM],
        out_specs=VMEM,
        scratch_shapes=[blocks],
        compiler_params=params(tiles, history, blocks, sums),
        name="multiply_own",
    )(table, tiles, history)


def multiply_tiles(first, whole, split, table, tiles, begun, received, after):
    halves, part, side = begun.shape
    chunks = halves // 2
    more = [jax.ShapeDtypeStruct((chunks // split * part + padded(chunks // split), side), jnp.int16)] * split
    blocks = pltpu.VMEM((table.shape[1], part, side), tiles.dtype)
    sums = jax.ShapeDtypeStruct(begun.shape, jnp.float32)
    return pl.pallas_call(
        functools.partial(tiles_kernel, first, whole, len(after), split),
        out_shape=[sums, *more],
        in_specs=[SMEM] + [VMEM] * (2 + len(received)) + [ANY] * len(after),
        out_specs=[VMEM] * (1 + split),
        scratch_shapes=[blocks],
        compiler_params=params(tiles, begun, *received, *more, blocks, sums),
        name="multiply_tiles",
    )(table, tiles, begun, *received, *after)


def to_fixed(value):
    largest = jnp.maximum(jnp.max(jnp.abs(value), axis=0, keepdims=True), 1e-30)
    exponent = jnp.ceil(jnp.log2(largest))
    grid = jnp.clip(jnp.round(value * jnp.exp2(15.0 - exponent)), -32767.0, 32767.0)
    return grid.astype(jnp.int32).astype(jnp.int16), exponent


def from_fixed(grid, exponent):
    return grid.astype(jnp.int32).astype(jnp.float32) * jnp.exp2(exponent - 15.0)


def code_kernel(per_owner, split, given, kept, *refs):
    got, own, coded, theirs = refs[:split], refs[split], refs[split + 1 : -1], refs[-1]
    chunks, part, side = theirs.shape
    size = chunks // split
    flag = given[given.shape[0] - PAD :, :].astype(jnp.int32).astype(jnp.float32)[PAD - 1 :, :LANES]
    for index, source in enumerate(got):
        tail = source[size * part :, :].astype(jnp.int32).astype(jnp.float32)
        flag = jnp.maximum(flag, tail[padded(size) - 1 :, :LANES])
        for chunk in range(size):
            theirs[index * size + chunk] = from_fixed(
                source[chunk * part : (chunk + 1) * part, :], tail[chunk : chunk + 1, :]
            )
    col = lax.axis_index("col")
    for step in list(range(1, chunks // per_owner)) + [0]:
        chunk = lax.bitwise_xor(col, step) * per_owner
        exponents = []
        for block in range(per_owner):
            value = kept[chunk + block] + theirs[chunk + block]
            if step == 0:
                own[block] = value
                continue
            out = coded[step - 1]
            grid, exponent = to_fixed(value)
            for lane in range(side // LANES):
                at = len(exponents)
                out[pl.ds(at * part, part), :] = grid[:, lane * LANES : (lane + 1) * LANES]
                exponents.append(exponent[:, lane * LANES : (lane + 1) * LANES])
        if step > 0:
            at = len(exponents)
            exponents.append(jnp.zeros((PAD - 1 - at, LANES), jnp.float32))
            exponents.append(flag)
            tail = jnp.concatenate(exponents, axis=0)
            out[pl.ds(at * part, PAD), :] = tail.astype(jnp.int32).astype(jnp.int16)


def code(given, kept, got, per_owner):
    chunks, part, side = kept.shape
    chunks = chunks // 2
    chunk = jax.ShapeDtypeStruct((per_owner * part * (side // LANES) + PAD, LANES), jnp.int16)
    own = jax.ShapeDtypeStruct((per_owner, part, side), jnp.float32)
    outs = [own] + [chunk] * (chunks // per_owner - 1)
    return pl.pallas_call(
        functools.partial(code_kernel, per_owner, len(got)),
        out_shape=outs,
        in_specs=[VMEM] * (2 + len(got)),
        out_specs=[VMEM] * len(outs),
        scratch_shapes=[pltpu.VMEM((chunks, part, side), jnp.float32)],
        compiler_params=params(given, kept, kept, *got, *outs),
        name="add_and_code",
    )(given, kept, *got)


def solve_kernel(first, fresh, *refs):
    refs, (stress_out, rate_out, stress_held, rate_held, sems) = refs[:-5], refs[-5:]
    if fresh:
        table, *refs, flag_out = refs
    else:
        refs = refs[2:]
    base, rate, direct, state, own, *codes = refs
    per_owner, part, side = own.shape
    rows = pl.ds(first, part)
    tails = [chunk[pl.ds(chunk.shape[0] - PAD, PAD), :].astype(jnp.int32).astype(jnp.float32) for chunk in codes]
    if fresh:
        flag = table[4, OVER].astype(jnp.float32)
        for tail in tails:
            flag = jnp.maximum(flag, jnp.max(tail[PAD - 1 :, :]))
        flag_out[0] = flag.astype(jnp.int32)
    count = per_owner * (side // LANES)
    copies = []
    for at in range(count):
        block, lane = at // (side // LANES), at % (side // LANES)
        stress = own[block, :, pl.ds(lane * LANES, LANES)]
        for chunk, tail in zip(codes, tails):
            stress = stress + from_fixed(chunk[pl.ds(at * part, part), :], tail[at : at + 1, :])
        stress_held[:, pl.ds(at * LANES, LANES)] = stress
    copies.append(pltpu.make_async_copy(stress_held, stress_out.at[rows], sems.at[0]))
    copies[-1].start()
    for at in range(count):
        lanes = pl.ds(at * LANES, LANES)
        rate_held[:, lanes] = friction(
            stress_held[:, lanes], base[rows, lanes], rate[rows, lanes], direct[rows, lanes], state[rows, lanes]
        )
    copies.append(pltpu.make_async_copy(rate_held, rate_out.at[rows], sems.at[1]))
    copies[-1].start()
    for copy in copies:
        copy.wait()


def solve(first, table, fields, own, coded, before):
    sims, owned = fields[0].shape
    part = own.shape[1]
    fresh = before is None
    field = jax.ShapeDtypeStruct(fields[0].shape, jnp.float32)
    held = pltpu.VMEM((part, owned), jnp.float32)
    flag = [jax.ShapeDtypeStruct((1,), jnp.int32)] if fresh else []
    results = pl.pallas_call(
        functools.partial(solve_kernel, first, fresh),
        out_shape=flag + [field, field],
        in_specs=([SMEM] if fresh else [ANY, ANY]) + [VMEM] * (5 + len(coded)),
        out_specs=[SMEM] * len(flag) + [ANY, ANY],
        input_output_aliases={} if fresh else {0: 0, 1: 1},
        scratch_shapes=[held, held, pltpu.SemaphoreType.DMA((2,))],
        compiler_params=params(*fields, own, held, held, *coded),
        name="friction_solve",
    )(*([table] if fresh else before), *fields, own, *coded)
    return results[:-2], results[-2:]


def reduce(first, table, fields, kept, given, before):
    per_owner = fields[0].shape[1] // kept.shape[2]
    col_size = lax.axis_size("col")
    got = [lax.ppermute(array, "lag", partners(lax.axis_size("lag"), 1)) for array in given]
    own, *coded = code(given[0], kept, got, per_owner)
    arrived = [
        lax.ppermute(coded[step - 1], "col", partners(col_size, step)) for step in [*range(2, col_size), 1]
    ]
    return solve(first, table, fields, own, arrived, before), (arrived[0], arrived[1]), tuple(arrived)


def local(history, kernel_tiles, tile_rows, tile_cols, tile_count, base_stress, prev_rate, direct_effect, state_var):
    _, _, lags, slots, side, _ = kernel_tiles.shape
    row_size, col_size = (lax.axis_size(axis) for axis in ("row", "col"))
    history = history[:, 0]
    tiles = kernel_tiles[0, 0]
    sims = history.shape[1]
    pieces = []
    for eighths in PIECES:
        pieces.append((sum(part for _, part in pieces), sims * eighths // 8))
    local_blocks = history.shape[2] // side
    total = row_size * local_blocks
    per_owner = base_stress.shape[1] // side
    chunks = col_size * per_owner
    cap = min(CAP, lags * local_blocks)
    fields = (base_stress, prev_rate, direct_effect, state_var)

    need = make_request(tile_cols, tile_count, total)
    requests = [lax.ppermute(need, "row", partners(row_size, step)) for step in range(1, row_size)]
    held = load(history)
    table, live_tiles = make_plan(
        tile_cols, tile_rows, tile_count, [need, *requests], tiles, cap, col_size, per_owner
    )

    begun = [multiply_own(first, part, table, live_tiles, held, chunks) for first, part in pieces]
    received = []
    for piece in pieces:
        after = (received[-1][0], *begun) if received else ()
        packed = pack(requests, held, side, cap, piece, after)
        received.append(
            [lax.ppermute(packed[step - 1], "row", partners(row_size, step)) for step in range(1, row_size)]
        )

    after = ()
    flags = result = None
    for (first, part), blocks, own in zip(pieces, received, begun):
        kept, *given = multiply_tiles(
            first, False, 1 if first + part == sims else SPLIT, table, live_tiles, multiply_early(table, live_tiles, own, blocks[0]), blocks[1:], after
        )
        (flag, result), after, _ = reduce(first, table, fields, kept, given, result)
        flags = flags or flag

    def general():
        everything = [lax.ppermute(history, "row", partners(row_size, step)) for step in range(1, row_size)]
        own = multiply_own(0, sims, table, live_tiles, history, chunks)
        kept, *given = multiply_tiles(
            0, True, 1, table, live_tiles, own, everything, ()
        )
        return tuple(reduce(0, table, fields, kept, given, None)[0][1])

    return lax.cond(flags[0][0] > 0, general, lambda: tuple(result))


def solution(mesh):
    return jax.shard_map(
        local,
        mesh=mesh,
        in_specs=(
            P("lag", "col", None, "row"),
            P("row", "col", "lag", None, None, None),
            P("row", "col", "lag", None),
            P("row", "col", "lag", None),
            P("row", "col", "lag"),
            P(None, ("row", "col", "lag")),
            P(None, ("row", "col", "lag")),
            P(None, ("row", "col", "lag")),
            P(None, ("row", "col", "lag")),
        ),
        out_specs=(P(None, ("row", "col", "lag")), P(None, ("row", "col", "lag"))),
        check_vma=False,
    )
```
